32 devices in a mesh: seq: 8 (over y, x, core), head: 4 (over z).
Axes of the slice: x: 2, y: 2, z: 4, core: 2. Of those that a mesh axis runs over, the one named last changes fastest.
Arguments:
- query_rows: bfloat16 [256, 512], P('seq', 'head'), may hold values from -6 to 6
- key_rows: bfloat16 [4096, 512], P('seq', 'head'), may hold values from -6 to 6
- value_rows: bfloat16 [4096, 512], P('seq', 'head'), may hold values from -6 to 6
- attn_out: bfloat16 [256, 512], P(('seq', 'head')), may hold values from -3 to 3
- out_grad: bfloat16 [256, 512], P(('seq', 'head')), may hold values from -48 to 48
- logsumexp: bfloat16 [4, 256], P('head', 'seq'), may hold values from 4.5 to 6.5
- shard_pick: int32 [4, 256, 4], P('head', 'seq'), may hold values from 0 to 7, all different within a row; in each aligned block of 32 rows (0 to 31, 32 to 63, ..., all dimensions but the last counted through in order) at most 32 rows name the same one
- block_pick: int32 [4, 256, 4, 4], P('head', 'seq'), may hold values from 0 to 7, as said below
Outputs:
- query_grad: bfloat16 [256, 512], P('seq', 'head')
- key_grad: bfloat16 [4096, 512], P('seq', 'head')
- value_grad: bfloat16 [4096, 512], P('seq', 'head')
The draws below stay inside these ranges and needn't reach their ends.
Inputs may be any that keep to these rules, and one draw needn't show every extreme that they name: `shard_pick`: each query row of each head names 4 different shards; among the 32 rows of one device (one head, one shard of query rows) no shard is named more than 32 times. `block_pick`: the 4 entries of one query row, head and group are different.
All inputs are finite; a program needn't handle non-finite values.
Results may differ from the reference program's by a relative error of at most 0.0077.
Values may be sent and summed in bfloat16 or wider, within the bound.
No kernel may reach another device: no remote copies, remote signals or barrier semaphores. Data moves between devices by JAX's collectives and lax.ppermute only.
A program may use at most 64 MiB of HBM per device.

```python
import math
import jax
import jax.numpy as jnp
import numpy as np
from jax import lax

DH = 128
HEADS = 4
BLK = 64
TOPK = 16
GROUPS = 4
PER_GROUP = 4
Q_DEV = 32
QROWS = 256
KEYS = 4096
BLOCKS_DEV = 8
CAP = 32
N_SEQ = 8


def draw_block_pick(key, part):
    scores = jax.random.randint(key, (HEADS, QROWS, GROUPS, BLOCKS_DEV), 0, 1 << 20, dtype=jnp.int32)
    scores = scores * BLOCKS_DEV + jnp.arange(BLOCKS_DEV, dtype=jnp.int32)
    return lax.top_k(scores, PER_GROUP)[1].astype(jnp.int32)


def shard_levels(stream_key, shape, shards, smallest, high):
    loudness, own = 1.0, jax.random.fold_in(stream_key, 6)
    for dim, shards_of in shards:
        draws = jnp.exp(jax.random.uniform(jax.random.fold_in(own, dim), (shards_of,), jnp.float32, smallest / len(shards), high / len(shards)))
        loudness = loudness * jnp.repeat(draws, shape[dim] // shards_of).reshape([-1 if axis == dim else 1 for axis in range(len(shape))])
    return loudness


def assign_block(key, own, number, rows, count, top, reach, lean):
    sequence = jax.random.permutation(key, count)
    crowded, common = shares(count, rows * top, reach, lean, True), shares(count, rows * top, reach, lean, False)
    places = jnp.arange(count)

    def named(tallies, offset_by):
        used = int((tallies > 0).sum())
        fixed = max(1, used // 4)
        shifted = fixed + (places - fixed + offset_by * (used - fixed)) % max(1, count - fixed)
        return jnp.zeros((count,), jnp.int32).at[sequence[jnp.where(places < fixed, places, shifted)]].set(jnp.asarray(tallies, jnp.int32))

    tallies = jnp.where(number % 4 == 0, named(crowded, number // 4), named(common, number - number // 4 - 1))
    mixed = jax.random.permutation(jax.random.fold_in(own, 3), count)
    source_of, sink = mixed[0:count // 2 * 2:2], mixed[1:count // 2 * 2:2]
    margin = jnp.minimum(tallies[source_of] - 1, reach - tallies[sink]) // 2
    margin = jnp.where((source_of == sequence[0]) | (sink == sequence[0]) | (tallies[sink] == 0), 0, jnp.maximum(margin, 0))
    shifted = jax.random.randint(jax.random.fold_in(own, 4), (count // 2,), 0, 1 << 20) % (margin + 1)
    tallies = tallies.at[source_of].add(-shifted).at[sink].add(shifted)
    items = jnp.searchsorted(jnp.cumsum(tallies), jnp.arange(rows * top), side="right").astype(jnp.int32)
    listing = items.reshape(top, rows).T
    listing = listing[jax.random.permutation(jax.random.fold_in(own, 1), rows)]
    offset_by = jax.random.randint(jax.random.fold_in(own, 2), (rows, 1), 0, top)
    return jnp.take_along_axis(listing, (jnp.arange(top)[None, :] + offset_by) % top, axis=1)


def shares(count, total, reach, skew, full):
    portions = [(1 << 20) // math.isqrt(standing ** skew) + 1 for standing in range(1, count + 1)]
    largest = reach if full else min(reach, max(-(-total // count), total * portions[0] // sum(portions)))
    least = 1 if total - largest >= count - 1 else 0
    holding, spare = [largest] + [least] * (count - 1), total - largest - least * (count - 1)
    while spare > 0:
        candidates = [i for i in range(1, count) if holding[i] < largest] or [i for i in range(1, count) if holding[i] < reach]
        whole, left = sum([portions[i] for i in candidates]), spare
        for i in candidates:
            extra = min(reach - holding[i], max(1, left * portions[i] // whole), spare)
            holding[i] = holding[i] + extra
            spare = spare - extra
    return np.array(holding)


def scatter_about(rng, dims, spread, limit, split=(), kind=jnp.bfloat16):
    loudness = shard_levels(rng, dims, split, -0.22, 0.18) if split else 1.0
    entries = jax.random.normal(rng, dims, jnp.float32) * spread * loudness
    return jnp.minimum(jnp.maximum(entries, -limit), limit).astype(kind)


def setup_inputs(seed: int = 0) -> dict:
    seeds = jax.random.split(jax.random.key(seed), 9)
    query_rows = scatter_about(seeds[0], (QROWS, HEADS * DH), 1.0, 6.0, ((0, 8), (1, 4)))
    key_rows = scatter_about(seeds[1], (KEYS, HEADS * DH), 1.0, 6.0, ((0, 8), (1, 4)))
    value_rows = scatter_about(seeds[2], (KEYS, HEADS * DH), 1.0, 6.0, ((0, 8), (1, 4)))
    attn_out = scatter_about(seeds[3], (QROWS, HEADS * DH), 0.5, 3.0, ((0, 32),))
    out_grad = scatter_about(seeds[4], (QROWS, HEADS * DH), 8.0, 48.0, ((0, 32),))
    logsumexp = jnp.clip(4.5 + 2.0 * jax.random.uniform(seeds[5], (HEADS, QROWS), jnp.float32) ** shard_levels(seeds[5], (HEADS, QROWS), ((0, 4), (1, 8)), -0.2, 0.2), 4.5, 6.5).astype(jnp.bfloat16)
    shard_pick_keys = jax.random.split(jax.random.fold_in(seeds[6], 1), HEADS * QROWS // Q_DEV)
    shard_pick_turns = jax.random.permutation(jax.random.fold_in(seeds[6], 3), HEADS * QROWS // Q_DEV)
    shard_pick = jax.vmap(lambda own, number: assign_block(jax.random.fold_in(seeds[6], 2), own, number, Q_DEV, N_SEQ, GROUPS, CAP, 2))(shard_pick_keys, shard_pick_turns).reshape((HEADS, QROWS, GROUPS))
    block_pick = draw_block_pick(jax.random.fold_in(seeds[8], 71), 0)
    return dict(query_rows=query_rows, key_rows=key_rows, value_rows=value_rows, attn_out=attn_out, out_grad=out_grad, logsumexp=logsumexp, shard_pick=shard_pick, block_pick=block_pick)


def head_grads(pieces):
    q_head, k_head, v_head, g_head, lse_head, delta_head, shard_head, pick_head = pieces
    scale = DH ** -0.5
    blocks = (shard_head[:, :, None] * BLOCKS_DEV + pick_head).reshape(QROWS, TOPK).astype(jnp.int32)
    all_blocks = jnp.arange(N_SEQ * BLOCKS_DEV, dtype=jnp.int32)
    chosen = jnp.any(blocks[:, :, None] == all_blocks[None, None, :], axis=1)
    mask = jnp.repeat(chosen, BLK, axis=1)
    scores = jnp.dot(q_head, k_head.T, preferred_element_type=jnp.float32) * scale
    probs = jnp.where(mask, jnp.exp(scores - lse_head.astype(jnp.float32)[:, None]), jnp.zeros_like(scores))
    probs_low = probs.astype(jnp.bfloat16)
    value_part = jnp.dot(probs_low.T, g_head, preferred_element_type=jnp.float32)
    dprob = jnp.dot(g_head, v_head.T, preferred_element_type=jnp.float32)
    dscore = (probs * (dprob - delta_head.astype(jnp.float32)[:, None])).astype(jnp.bfloat16)
    query_part = jnp.dot(dscore, k_head, preferred_element_type=jnp.float32) * scale
    key_part = jnp.dot(dscore.T, q_head, preferred_element_type=jnp.float32) * scale
    return query_part.astype(jnp.bfloat16), key_part.astype(jnp.bfloat16), value_part.astype(jnp.bfloat16)


def reference(query_rows, key_rows, value_rows, attn_out, out_grad, logsumexp, shard_pick, block_pick):
    delta = (attn_out.astype(jnp.float32) * out_grad.astype(jnp.float32)).reshape(QROWS, HEADS, DH).sum(axis=2)
    delta = lax.optimization_barrier(delta.astype(jnp.bfloat16))
    q_heads = query_rows.reshape(QROWS, HEADS, DH).transpose(1, 0, 2)
    k_heads = key_rows.reshape(KEYS, HEADS, DH).transpose(1, 0, 2)
    v_heads = value_rows.reshape(KEYS, HEADS, DH).transpose(1, 0, 2)
    g_heads = out_grad.reshape(QROWS, HEADS, DH).transpose(1, 0, 2)
    query_grad, key_grad, value_grad = lax.map(head_grads, (q_heads, k_heads, v_heads, g_heads, logsumexp, delta.T, shard_pick, block_pick))
    query_grad = query_grad.transpose(1, 0, 2).reshape(QROWS, HEADS * DH)
    key_grad = key_grad.transpose(1, 0, 2).reshape(KEYS, HEADS * DH)
    value_grad = value_grad.transpose(1, 0, 2).reshape(KEYS, HEADS * DH)
    return query_grad, key_grad, value_grad
```

```python
import functools

import jax
import jax.numpy as jnp
from jax import lax
from jax.experimental import pallas as pl
from jax.experimental.pallas import tpu as pltpu
from jax.sharding import PartitionSpec as P

BLK = 64
LOG2E = 1.4426950408889634


def block_terms(row_data, small_data, key_rows, value_rows, own_shard, groups):
    count = row_data.shape[0]
    head_size = key_rows.shape[1]
    per_shard = key_rows.shape[0] // BLK
    queries = row_data[:, :head_size]
    grads = row_data[:, head_size:]
    stats = small_data[:, :2].astype(jnp.float32)
    shards_of = small_data[:, 2 : 2 + groups].astype(jnp.int32)
    picks_of = small_data[:, 2 + groups :].astype(jnp.int32).reshape(count, groups, -1)
    local_ids = jnp.arange(per_shard, dtype=jnp.int32)
    matched = (shards_of == own_shard + 1)[:, :, None, None] & (
        picks_of[:, :, :, None] == local_ids[None, None, None, :]
    )
    chosen = jnp.any(matched, axis=(1, 2))
    mask = jnp.broadcast_to(chosen[:, :, None], (count, per_shard, BLK)).reshape(
        count, key_rows.shape[0]
    )
    scores = jnp.dot(queries, key_rows.T, preferred_element_type=jnp.float32) * head_size ** (-0.5)
    probs = jnp.where(mask, jnp.exp(scores - stats[:, 0:1]), 0.0)
    probs_low = probs.astype(jnp.bfloat16)
    value_add = jnp.dot(probs_low.T, grads, preferred_element_type=jnp.float32)
    dprob = jnp.dot(grads, value_rows.T, preferred_element_type=jnp.float32)
    dscore = (probs * (dprob - stats[:, 1:2])).astype(jnp.bfloat16)
    key_add = jnp.dot(dscore.T, queries, preferred_element_type=jnp.float32)
    query_part = jnp.dot(dscore, key_rows, preferred_element_type=jnp.float32)
    return (query_part, key_add, value_add)


def sweep(rows_in, small_in, key_rows, value_rows, own_shard, groups):
    sources, per_source = (rows_in.shape[0], rows_in.shape[1])
    merged = 1
    while merged * 2 <= sources and sources % (merged * 2) == 0 and (merged * per_source < 512):
        merged = merged * 2
    rows_blocks = rows_in.reshape(sources // merged, merged * per_source, rows_in.shape[2])
    small_blocks = small_in.reshape(sources // merged, merged * per_source, small_in.shape[2])
    zeros_kv = jnp.zeros(key_rows.shape, jnp.float32)

    def advance(carry, pieces):
        query_part, key_add, value_add = block_terms(
            pieces[0], pieces[1], key_rows, value_rows, own_shard, groups
        )
        return ((carry[0] + key_add, carry[1] + value_add), query_part)

    (key_sum, value_sum), query_parts = lax.scan(
        advance, (zeros_kv, zeros_kv), (rows_blocks, small_blocks)
    )
    return (query_parts.reshape(sources, per_source, -1), key_sum, value_sum)


def general_local(query_rows, key_rows, value_rows, attn_out, out_grad, logsumexp, shard_pick, block_pick):
    head_size = query_rows.shape[1]
    q_count = query_rows.shape[0]
    scale = head_size ** (-0.5)
    out_local, grad_local = (
        lax.all_to_all(attn_out, "head", split_axis=1, concat_axis=0, tiled=True),
        lax.all_to_all(out_grad, "head", split_axis=1, concat_axis=0, tiled=True),
    )
    delta = jnp.sum(
        out_local.astype(jnp.float32) * grad_local.astype(jnp.float32), axis=1, keepdims=True
    ).astype(jnp.bfloat16)
    seq_count = lax.axis_size("seq")
    own_shard = lax.axis_index("seq")
    targets = shard_pick[0]
    groups = targets.shape[1]
    picks = block_pick[0].reshape(q_count, -1)
    row_data = jnp.concatenate([query_rows, grad_local], axis=1)
    small_data = jnp.concatenate(
        [
            logsumexp[0][:, None],
            delta,
            (targets + 1).astype(jnp.bfloat16),
            picks.astype(jnp.bfloat16),
        ],
        axis=1,
    )
    capacity = min(q_count, 2 * q_count * groups // seq_count)
    shard_ids = jnp.arange(seq_count, dtype=jnp.int32)
    hits = jnp.any(targets[:, :, None] == shard_ids[None, None, :], axis=1).astype(jnp.float32)
    row_ids = jnp.arange(q_count, dtype=jnp.int32)
    lower = (row_ids[:, None] >= row_ids[None, :]).astype(jnp.float32)
    slots = (
        jnp.dot(lower, hits, precision=lax.Precision.HIGHEST, preferred_element_type=jnp.float32)
        - 1.0
    )
    slot_ids = jnp.arange(capacity, dtype=jnp.float32)
    dispatch = hits.T[:, None, :] * (slots.T[:, None, :] == slot_ids[None, :, None]).astype(
        jnp.float32
    )
    dispatch_low = dispatch.astype(jnp.bfloat16)
    send_rows = jnp.einsum(
        "scr,rf->scf", dispatch_low, row_data, preferred_element_type=jnp.float32
    ).astype(jnp.bfloat16)
    send_small = jnp.einsum(
        "scr,rf->scf", dispatch_low, small_data, preferred_element_type=jnp.float32
    ).astype(jnp.bfloat16)
    got_rows, got_small = (
        lax.all_to_all(send_rows, "seq", split_axis=0, concat_axis=0, tiled=True),
        lax.all_to_all(send_small, "seq", split_axis=0, concat_axis=0, tiled=True),
    )
    query_parts, key_sum, value_sum = sweep(
        got_rows, got_small, key_rows, value_rows, own_shard, groups
    )
    returned = lax.all_to_all(query_parts, "seq", split_axis=0, concat_axis=0, tiled=True)
    total = jnp.einsum(
        "scr,scd->rd",
        dispatch,
        returned,
        precision=lax.Precision.HIGHEST,
        preferred_element_type=jnp.float32,
    )
    query_grad = (total * scale).astype(jnp.bfloat16)
    key_grad = (key_sum * scale).astype(jnp.bfloat16)
    value_grad = value_sum.astype(jnp.bfloat16)
    return (query_grad, key_grad, value_grad)


def swap(value, axis, count, bit):
    return lax.ppermute(value, axis, [(i, i ^ bit) for i in range(count)])


def attend(rows, picks, far, key_ref, value_ref, shard, scale):
    queries, grads = rows
    base = (shard * (key_ref.shape[0] // BLK)).astype(jnp.float32)
    blocks = key_ref.shape[0] // BLK
    stats, ids = picks
    number = lax.broadcasted_iota(jnp.int32, (blocks, ids.shape[1]), 0).astype(jnp.float32) + base
    chosen = ids[0:1] == number
    for k in range(1, ids.shape[0]):
        chosen = chosen | (ids[k : k + 1] == number)
    offset = jnp.where(chosen, stats[0:1] * LOG2E, far)
    delta = stats[1:2]
    keys, values = key_ref[...], value_ref[...]
    contract = (((1,), (1,)), ((), ()))
    scores = lax.dot_general(keys, queries, contract, preferred_element_type=jnp.float32)
    dprob = lax.dot_general(values, grads, contract, preferred_element_type=jnp.float32)
    scores = scores.reshape(blocks, BLK, -1)
    probs = jnp.exp2(scores * (scale * LOG2E) - offset[:, None, :]).reshape(dprob.shape)
    dscore = (probs * (dprob - delta)).astype(jnp.bfloat16)
    probs_low = probs.astype(jnp.bfloat16)
    value_add = jnp.dot(probs_low, grads, preferred_element_type=jnp.float32)
    key_add = jnp.dot(dscore, queries, preferred_element_type=jnp.float32)
    query_add = lax.dot_general(
        dscore, keys, (((0,), (0,)), ((), ())), preferred_element_type=jnp.float32
    )
    return query_add, key_add, value_add


def core_kernel(
    scale, shard_ref, r0, r1, r2, r3, k0, v0, k1, v1, q_own, q_out, k_own, v_own, k_out, v_out
):
    count = q_own.shape[0]
    parts = (r0, r1, r2, r3)
    queries = jnp.concatenate([r[0:count] for r in parts], axis=0)
    grads = jnp.concatenate([r[count : 2 * count] for r in parts], axis=0)
    small = [r[2 * count :].astype(jnp.float32) for r in parts]
    lane = lax.broadcasted_iota(jnp.int32, small[0].shape, 1) // count
    merged = small[0]
    for k in range(1, len(parts)):
        merged = jnp.where(lane == k, small[k], merged)
    half = merged.shape[0] // 2
    picks = (merged[:half], merged[half:])
    shard = shard_ref[0]
    q_a, k_a, v_a = attend((queries, grads), picks, 1e30, k1, v1, shard ^ 1, scale)
    k_out[...] = k_a.astype(k_out.dtype)
    v_out[...] = v_a.astype(v_out.dtype)
    q_b, k_b, v_b = attend((queries, grads), picks, 1e30, k0, v0, shard, scale)
    k_own[...] = k_b
    v_own[...] = v_b
    q_all = q_a + q_b
    q_own[...] = q_all[:count]
    for k in range(1, len(parts)):
        q_out[k - 1] = q_all[k * count : (k + 1) * count].astype(q_out.dtype)


def fast_local(query_rows, key_rows, value_rows, attn_out, out_grad, logsumexp, shard_pick, block_pick):
    count, size = query_rows.shape
    n_seq, n_head = lax.axis_size("seq"), lax.axis_size("head")
    seq, head = lax.axis_index("seq"), lax.axis_index("head")
    scale = size ** (-0.5)
    grad_near = swap(out_grad, "head", n_head, 1)
    out_near = swap(attn_out, "head", n_head, 1)
    keys_near = swap(key_rows, "seq", n_seq, 1)
    values_near = swap(value_rows, "seq", n_seq, 1)

    def columns(value, which):
        return lax.dynamic_slice_in_dim(value, which * size, size, axis=1)

    def pieces(which):
        return jnp.stack([columns(v, which) for v in (out_grad, grad_near, attn_out, out_near)])

    near = pieces(head)
    other = swap(pieces(head ^ 2), "head", n_head, 2)
    odd, high = (head & 1) == 1, (head & 2) == 2

    def ordered(a, b, c, d):
        a, b = jnp.where(odd, b, a), jnp.where(odd, a, b)
        c, d = jnp.where(odd, d, c), jnp.where(odd, c, d)
        low, top = jnp.concatenate([a, b]), jnp.concatenate([c, d])
        return jnp.concatenate([jnp.where(high, top, low), jnp.where(high, low, top)])

    grads = ordered(near[0], near[1], other[0], other[1])
    outs = ordered(near[2], near[3], other[2], other[3])
    delta = jnp.sum(outs.astype(jnp.float32) * grads.astype(jnp.float32), axis=1).astype(jnp.bfloat16)
    blocks_dev = key_rows.shape[0] // BLK
    ids = shard_pick[0][:, :, None] * blocks_dev + block_pick[0]
    ids = ids.reshape(count, -1).T.astype(jnp.bfloat16)
    top = ids.shape[0]
    stats = jnp.concatenate(
        [logsumexp, delta[None, :], jnp.zeros((top - 2, count), jnp.bfloat16)], axis=0
    )
    small = jnp.tile(jnp.concatenate([stats, ids], axis=0), (1, size // count))
    block = jnp.concatenate([query_rows, grads, small], axis=0)
    bits = (2, 4, 6)
    others = [swap(block, "seq", n_seq, bit) for bit in bits]
    f32, bf16 = jnp.float32, jnp.bfloat16
    kv = key_rows.shape
    vmem = pl.BlockSpec(memory_space=pltpu.VMEM)
    q_own, q_out, k_own, v_own, k_out, v_out = pl.pallas_call(
        functools.partial(core_kernel, scale),
        out_shape=(
            jax.ShapeDtypeStruct((count, size), f32),
            jax.ShapeDtypeStruct((len(bits), count, size), bf16),
            jax.ShapeDtypeStruct(kv, f32),
            jax.ShapeDtypeStruct(kv, f32),
            jax.ShapeDtypeStruct(kv, bf16),
            jax.ShapeDtypeStruct(kv, bf16),
        ),
        in_specs=[pl.BlockSpec(memory_space=pltpu.SMEM)] + [vmem] * 8,
        out_specs=(vmem,) * 6,
        compiler_params=pltpu.CompilerParams(vmem_limit_bytes=32 * 1024 * 1024),
        name="block_terms",
    )(seq[None].astype(jnp.int32), block, *others, key_rows, value_rows, keys_near, values_near)
    back = [swap(q_out[k], "seq", n_seq, bit) for k, bit in enumerate(bits)]
    k_back = swap(k_out, "seq", n_seq, 1)
    v_back = swap(v_out, "seq", n_seq, 1)
    total = q_own + sum(part.astype(f32) for part in back)
    query_grad = (total * scale).astype(bf16)
    key_grad = ((k_own + k_back.astype(f32)) * scale).astype(bf16)
    value_grad = (v_own + v_back.astype(f32)).astype(bf16)
    return query_grad, key_grad, value_grad


def solution(mesh):
    placed = (
        P("seq", "head"),
        P("seq", "head"),
        P("seq", "head"),
        P(("seq", "head"), None),
        P(("seq", "head"), None),
        P("head", "seq"),
        P("head", "seq", None),
        P("head", "seq", None, None),
    )
    small = mesh.shape["seq"] == 8 and mesh.shape["head"] == 4

    def local(*args):
        count, size = args[0].shape
        fits = small and count * 4 == size == 128 and args[7].shape[2] * args[7].shape[3] == 16
        return (fast_local if fits else general_local)(*args)

    return jax.shard_map(
        local,
        mesh=mesh,
        in_specs=placed,
        out_specs=(P("seq", "head"), P("seq", "head"), P("seq", "head")),
        check_vma=False,
    )
```

```python
import functools

import jax
import jax.numpy as jnp
from jax import lax
from jax.experimental import pallas as pl
from jax.experimental.pallas import tpu as pltpu
from jax.sharding import PartitionSpec as P

BLK = 64
LOG2E = 1.4426950408889634


def block_terms(row_data, small_data, key_rows, value_rows, own_shard, groups):
    count = row_data.shape[0]
    head_size = key_rows.shape[1]
    per_shard = key_rows.shape[0] // BLK
    queries = row_data[:, :head_size]
    grads = row_data[:, head_size:]
    stats = small_data[:, :2].astype(jnp.float32)
    shards_of = small_data[:, 2 : 2 + groups].astype(jnp.int32)
    picks_of = small_data[:, 2 + groups :].astype(jnp.int32).reshape(count, groups, -1)
    local_ids = jnp.arange(per_shard, dtype=jnp.int32)
    matched = (shards_of == own_shard + 1)[:, :, None, None] & (
        picks_of[:, :, :, None] == local_ids[None, None, None, :]
    )
    chosen = jnp.any(matched, axis=(1, 2))
    mask = jnp.broadcast_to(chosen[:, :, None], (count, per_shard, BLK)).reshape(
        count, key_rows.shape[0]
    )
    scores = jnp.dot(queries, key_rows.T, preferred_element_type=jnp.float32) * head_size ** (-0.5)
    probs = jnp.where(mask, jnp.exp(scores - stats[:, 0:1]), 0.0)
    probs_low = probs.astype(jnp.bfloat16)
    value_add = jnp.dot(probs_low.T, grads, preferred_element_type=jnp.float32)
    dprob = jnp.dot(grads, value_rows.T, preferred_element_type=jnp.float32)
    dscore = (probs * (dprob - stats[:, 1:2])).astype(jnp.bfloat16)
    key_add = jnp.dot(dscore.T, queries, preferred_element_type=jnp.float32)
    query_part = jnp.dot(dscore, key_rows, preferred_element_type=jnp.float32)
    return (query_part, key_add, value_add)


def sweep(rows_in, small_in, key_rows, value_rows, own_shard, groups):
    sources, per_source = (rows_in.shape[0], rows_in.shape[1])
    merged = 1
    while merged * 2 <= sources and sources % (merged * 2) == 0 and (merged * per_source < 512):
        merged = merged * 2
    rows_blocks = rows_in.reshape(sources // merged, merged * per_source, rows_in.shape[2])
    small_blocks = small_in.reshape(sources // merged, merged * per_source, small_in.shape[2])
    zeros_kv = jnp.zeros(key_rows.shape, jnp.float32)

    def advance(carry, pieces):
        query_part, key_add, value_add = block_terms(
            pieces[0], pieces[1], key_rows, value_rows, own_shard, groups
        )
        return ((carry[0] + key_add, carry[1] + value_add), query_part)

    (key_sum, value_sum), query_parts = lax.scan(
        advance, (zeros_kv, zeros_kv), (rows_blocks, small_blocks)
    )
    return (query_parts.reshape(sources, per_source, -1), key_sum, value_sum)


def general_local(query_rows, key_rows, value_rows, attn_out, out_grad, logsumexp, shard_pick, block_pick):
    head_size = query_rows.shape[1]
    q_count = query_rows.shape[0]
    scale = head_size ** (-0.5)
    out_local, grad_local = (
        lax.all_to_all(attn_out, "head", split_axis=1, concat_axis=0, tiled=True),
        lax.all_to_all(out_grad, "head", split_axis=1, concat_axis=0, tiled=True),
    )
    delta = jnp.sum(
        out_local.astype(jnp.float32) * grad_local.astype(jnp.float32), axis=1, keepdims=True
    ).astype(jnp.bfloat16)
    seq_count = lax.axis_size("seq")
    own_shard = lax.axis_index("seq")
    targets = shard_pick[0]
    groups = targets.shape[1]
    picks = block_pick[0].reshape(q_count, -1)
    row_data = jnp.concatenate([query_rows, grad_local], axis=1)
    small_data = jnp.concatenate(
        [
            logsumexp[0][:, None],
            delta,
            (targets + 1).astype(jnp.bfloat16),
            picks.astype(jnp.bfloat16),
        ],
        axis=1,
    )
    capacity = min(q_count, 2 * q_count * groups // seq_count)
    shard_ids = jnp.arange(seq_count, dtype=jnp.int32)
    hits = jnp.any(targets[:, :, None] == shard_ids[None, None, :], axis=1).astype(jnp.float32)
    row_ids = jnp.arange(q_count, dtype=jnp.int32)
    lower = (row_ids[:, None] >= row_ids[None, :]).astype(jnp.float32)
    slots = (
        jnp.dot(lower, hits, precision=lax.Precision.HIGHEST, preferred_element_type=jnp.float32)
        - 1.0
    )
    slot_ids = jnp.arange(capacity, dtype=jnp.float32)
    dispatch = hits.T[:, None, :] * (slots.T[:, None, :] == slot_ids[None, :, None]).astype(
        jnp.float32
    )
    dispatch_low = dispatch.astype(jnp.bfloat16)
    send_rows = jnp.einsum(
        "scr,rf->scf", dispatch_low, row_data, preferred_element_type=jnp.float32
    ).astype(jnp.bfloat16)
    send_small = jnp.einsum(
        "scr,rf->scf", dispatch_low, small_data, preferred_element_type=jnp.float32
    ).astype(jnp.bfloat16)
    got_rows, got_small = (
        lax.all_to_all(send_rows, "seq", split_axis=0, concat_axis=0, tiled=True),
        lax.all_to_all(send_small, "seq", split_axis=0, concat_axis=0, tiled=True),
    )
    query_parts, key_sum, value_sum = sweep(
        got_rows, got_small, key_rows, value_rows, own_shard, groups
    )
    returned = lax.all_to_all(query_parts, "seq", split_axis=0, concat_axis=0, tiled=True)
    total = jnp.einsum(
        "scr,scd->rd",
        dispatch,
        returned,
        precision=lax.Precision.HIGHEST,
        preferred_element_type=jnp.float32,
    )
    query_grad = (total * scale).astype(jnp.bfloat16)
    key_grad = (key_sum * scale).astype(jnp.bfloat16)
    value_grad = value_sum.astype(jnp.bfloat16)
    return (query_grad, key_grad, value_grad)


def swap(value, axis, count, bit):
    return lax.ppermute(value, axis, [(i, i ^ bit) for i in range(count)])


def row_sums(left, right):
    product = left.astype(jnp.float32) * right.astype(jnp.float32)
    high = product.astype(jnp.bfloat16)
    low = (product - high.astype(jnp.float32)).astype(jnp.bfloat16)
    ones = jnp.ones((8, product.shape[1]), jnp.bfloat16)
    contract = (((1,), (1,)), ((), ()))
    total = lax.dot_general(ones, high, contract, preferred_element_type=jnp.float32)
    total = total + lax.dot_general(ones, low, contract, preferred_element_type=jnp.float32)
    return total[0:1]


def unpack(parts, count):
    queries, grads, outs = (
        jnp.concatenate([r[k * count : (k + 1) * count] for r in parts], axis=0) for k in range(3)
    )
    small = [r[3 * count :].astype(jnp.float32) for r in parts]
    lane = lax.broadcasted_iota(jnp.int32, small[0].shape, 1) // count
    merged = small[0]
    for k in range(1, len(parts)):
        merged = jnp.where(lane == k, small[k], merged)
    merged = merged[:, : queries.shape[0]]
    half = merged.shape[0] // 2
    delta = row_sums(outs, grads).astype(jnp.bfloat16).astype(jnp.float32)
    return queries, grads, delta, merged[0:1], merged[half:]


def terms(rows, keys, values, base, scale):
    queries, grads, delta, lse, ids = rows
    blocks = keys.shape[0] // BLK
    number = lax.broadcasted_iota(jnp.int32, (blocks, ids.shape[1]), 0) + base
    number = number.astype(jnp.float32)
    chosen = ids[0:1] == number
    for k in range(1, ids.shape[0]):
        chosen = chosen | (ids[k : k + 1] == number)
    offset = jnp.where(chosen, lse * LOG2E, 1e30)
    contract = (((1,), (1,)), ((), ()))
    scores = lax.dot_general(keys, queries, contract, preferred_element_type=jnp.float32)
    dprob = lax.dot_general(values, grads, contract, preferred_element_type=jnp.float32)
    scores = scores.reshape(blocks, BLK, -1)
    probs = jnp.exp2(scores * (scale * LOG2E) - offset[:, None, :]).reshape(dprob.shape)
    dscore = (probs * (dprob - delta)).astype(jnp.bfloat16)
    return probs.astype(jnp.bfloat16), dscore


def beside(value, half):
    row = lax.broadcasted_iota(jnp.int32, value.shape, 0)
    zero = jnp.zeros_like(value)
    return jnp.concatenate(
        [jnp.where(row < half, value, zero), jnp.where(row < half, zero, value)], axis=1
    )


def query_kernel(scale, shard_ref, r0, r1, *refs):
    count = r0.shape[0] // 4
    pairs, (q_own, q_out) = refs[:-2], refs[-2:]
    queries, grads, delta, lse, ids = unpack((r0[...], r1[...], r0[...], r1[...]), count)
    half, size = 2 * count, queries.shape[1]
    rows = (beside(queries, half), beside(grads, half), delta, lse, ids)
    lane = lax.broadcasted_iota(jnp.int32, (1, 2 * half), 1)
    total = None
    for k in range(0, len(pairs), 4):
        left, right = shard_ref[0] ^ (k // 2), shard_ref[0] ^ (k // 2 + 1)
        keys = jnp.concatenate([pairs[k][...], pairs[k + 2][...]], axis=1)
        values = jnp.concatenate([pairs[k + 1][...], pairs[k + 3][...]], axis=1)
        base = jnp.where(lane < half, left, right) * (keys.shape[0] // BLK)
        _, dscore = terms(rows, keys, values, base, scale)
        part = lax.dot_general(
            dscore, keys, (((0,), (0,)), ((), ())), preferred_element_type=jnp.float32
        )
        part = part[:half, :size] + part[half:, size:]
        total = part if total is None else total + part
    q_own[...] = total[:count]
    q_out[...] = total[count:].astype(q_out.dtype)


def key_sums(shard, lane, keys, values, scale):
    count = lane.shape[1] // 4
    rows = unpack([lane[k] for k in range(lane.shape[0])], count)
    base = shard * (keys.shape[0] // BLK)
    probs, dscore = terms(rows, keys[...], values[...], base, scale)
    v_sum = jnp.dot(probs, rows[1], preferred_element_type=jnp.float32)
    k_sum = jnp.dot(dscore, rows[0], preferred_element_type=jnp.float32)
    return k_sum, v_sum


def key_kernel(scale, shard_ref, lane, keys, values, k_part, v_part):
    k_part[...], v_part[...] = key_sums(shard_ref[0], lane, keys, values, scale)


def query_sum_kernel(scale, q_own, q_back, q_sum):
    q_sum[...] = ((q_own[...] + q_back[...].astype(jnp.float32)) * scale).astype(q_sum.dtype)


def finish_kernel(
    scale, shard_ref, lane, keys, values, k_part, v_part, q_sum, q_out, k_out, v_out
):
    k_sum, v_sum = key_sums(shard_ref[0], lane, keys, values, scale)
    k_out[...] = ((k_sum + k_part[...]) * scale).astype(k_out.dtype)
    v_out[...] = (v_sum + v_part[...]).astype(v_out.dtype)
    q_out[...] = q_sum[...]


def fast_local(query_rows, key_rows, value_rows, attn_out, out_grad, logsumexp, shard_pick, block_pick):
    count, size = query_rows.shape
    n_seq, n_head = lax.axis_size("seq"), lax.axis_size("head")
    seq, head = lax.axis_index("seq"), lax.axis_index("head")
    scale = size ** (-0.5)
    f32, bf16 = jnp.float32, jnp.bfloat16
    mine = jnp.stack([out_grad, attn_out])
    near = swap(mine, "head", n_head, 1)
    mine, keys, values = lax.optimization_barrier((mine, key_rows, value_rows))
    keys_side = swap(keys, "seq", n_seq, 2)
    values_side = swap(values, "seq", n_seq, 2)
    near, shard_pick, block_pick, query_rows, logsumexp = lax.optimization_barrier(
        (near, shard_pick, block_pick, query_rows, logsumexp)
    )

    def pieces(which):
        both = jnp.stack([mine, near], axis=1)
        return lax.dynamic_slice_in_dim(both, which * size, size, axis=3)

    here = pieces(head)
    other = swap(pieces(head ^ 2), "head", n_head, 2)
    near, keys, values = lax.optimization_barrier((near, key_rows, value_rows))
    keys_core = swap(keys, "seq", n_seq, 1)
    values_core = swap(values, "seq", n_seq, 1)
    keys_side_core = swap(keys_side, "seq", n_seq, 1)
    values_side_core = swap(values_side, "seq", n_seq, 1)
    blocks_dev = key_rows.shape[0] // BLK
    ids = shard_pick[0][:, :, None] * blocks_dev + block_pick[0]
    ids = ids.reshape(count, -1).T.astype(bf16)
    top = ids.shape[0]
    stats = jnp.concatenate([logsumexp, jnp.zeros((top - 1, count), bf16)], axis=0)
    small = jnp.tile(jnp.concatenate([stats, ids], axis=0), (1, size // count))
    early = jnp.concatenate([query_rows, small], axis=0)
    early, other = lax.optimization_barrier((early, other))
    odd, high = (head & 1) == 1, (head & 2) == 2
    both = jnp.stack([jnp.where(high, other, here), jnp.where(high, here, other)], axis=1)
    both = jnp.where(odd, both[:, :, ::-1], both)
    both = both.reshape(2 * count, size)
    block = jnp.concatenate([early[:count], both, early[count:]], axis=0)
    block, keys_core, values_core = lax.optimization_barrier((block, keys_core, values_core))
    block_y = swap(block, "seq", n_seq, 4)
    block_x = swap(block, "seq", n_seq, 2)
    block_d = swap(block, "seq", n_seq, 6)
    kv = key_rows.shape
    vmem = pl.BlockSpec(memory_space=pltpu.VMEM)
    smem = pl.BlockSpec(memory_space=pltpu.SMEM)
    params = pltpu.CompilerParams(vmem_limit_bytes=32 * 1024 * 1024)
    shard = seq[None].astype(jnp.int32)
    q_own, q_out = pl.pallas_call(
        functools.partial(query_kernel, scale),
        out_shape=(
            jax.ShapeDtypeStruct((count, size), f32),
            jax.ShapeDtypeStruct((count, size), bf16),
        ),
        in_specs=[smem] + [vmem] * 10,
        out_specs=(vmem,) * 2,
        compiler_params=params,
        name="query_terms",
    )(
        shard, block, block_y, key_rows, value_rows, keys_core, values_core,
        keys_side, values_side, keys_side_core, values_side_core,
    )
    _, block_x, block_d = lax.optimization_barrier((q_out, block_x, block_d))
    q_back = swap(q_out, "seq", n_seq, 4)
    lane = jnp.stack([block, block_y, block_x, block_d])
    lane_core = swap(lane, "seq", n_seq, 1)
    k_part, v_part = pl.pallas_call(
        functools.partial(key_kernel, scale),
        out_shape=(jax.ShapeDtypeStruct(kv, f32),) * 2,
        in_specs=[smem] + [vmem] * 3,
        out_specs=(vmem,) * 2,
        compiler_params=params,
        cost_estimate=pl.CostEstimate(flops=1, bytes_accessed=1, transcendentals=0),
        name="key_terms",
    )(shard, lane, key_rows, value_rows)
    q_sum = pl.pallas_call(
        functools.partial(query_sum_kernel, scale),
        out_shape=jax.ShapeDtypeStruct((count, size), bf16),
        in_specs=[vmem] * 2,
        out_specs=vmem,
        compiler_params=params,
        cost_estimate=pl.CostEstimate(flops=10**11, bytes_accessed=10**8, transcendentals=0),
        name="query_sum",
    )(q_own, q_back)
    return pl.pallas_call(
        functools.partial(finish_kernel, scale),
        out_shape=tuple(jax.ShapeDtypeStruct(v, bf16) for v in ((count, size), kv, kv)),
        in_specs=[smem] + [vmem] * 6,
        compiler_params=params,
        name="finish",
    )(shard, lane_core, key_rows, value_rows, k_part, v_part, q_sum)


def solution(mesh):
    placed = (
        P("seq", "head"),
        P("seq", "head"),
        P("seq", "head"),
        P(("seq", "head"), None),
        P(("seq", "head"), None),
        P("head", "seq"),
        P("head", "seq", None),
        P("head", "seq", None, None),
    )
    small = mesh.shape["seq"] == 8 and mesh.shape["head"] == 4

    def local(*args):
        count, size = args[0].shape
        fits = small and count * 4 == size == 128 and args[7].shape[2] * args[7].shape[3] == 16
        return (fast_local if fits else general_local)(*args)

    return jax.shard_map(
        local,
        mesh=mesh,
        in_specs=placed,
        out_specs=(P("seq", "head"), P("seq", "head"), P("seq", "head")),
        check_vma=False,
    )
```

```python
import functools

import jax
import jax.numpy as jnp
from jax import lax
from jax.experimental import pallas as pl
from jax.experimental.pallas import tpu as pltpu
from jax.sharding import PartitionSpec as P

BLK = 64
LOG2E = 1.4426950408889634


def block_terms(row_data, small_data, key_rows, value_rows, own_shard, groups):
    count = row_data.shape[0]
    head_size = key_rows.shape[1]
    per_shard = key_rows.shape[0] // BLK
    queries = row_data[:, :head_size]
    grads = row_data[:, head_size:]
    stats = small_data[:, :2].astype(jnp.float32)
    shards_of = small_data[:, 2 : 2 + groups].astype(jnp.int32)
    picks_of = small_data[:, 2 + groups :].astype(jnp.int32).reshape(count, groups, -1)
    local_ids = jnp.arange(per_shard, dtype=jnp.int32)
    matched = (shards_of == own_shard + 1)[:, :, None, None] & (
        picks_of[:, :, :, None] == local_ids[None, None, None, :]
    )
    chosen = jnp.any(matched, axis=(1, 2))
    mask = jnp.broadcast_to(chosen[:, :, None], (count, per_shard, BLK)).reshape(
        count, key_rows.shape[0]
    )
    scores = jnp.dot(queries, key_rows.T, preferred_element_type=jnp.float32) * head_size ** (-0.5)
    probs = jnp.where(mask, jnp.exp(scores - stats[:, 0:1]), 0.0)
    probs_low = probs.astype(jnp.bfloat16)
    value_add = jnp.dot(probs_low.T, grads, preferred_element_type=jnp.float32)
    dprob = jnp.dot(grads, value_rows.T, preferred_element_type=jnp.float32)
    dscore = (probs * (dprob - stats[:, 1:2])).astype(jnp.bfloat16)
    key_add = jnp.dot(dscore.T, queries, preferred_element_type=jnp.float32)
    query_part = jnp.dot(dscore, key_rows, preferred_element_type=jnp.float32)
    return (query_part, key_add, value_add)


def sweep(rows_in, small_in, key_rows, value_rows, own_shard, groups):
    sources, per_source = (rows_in.shape[0], rows_in.shape[1])
    merged = 1
    while merged * 2 <= sources and sources % (merged * 2) == 0 and (merged * per_source < 512):
        merged = merged * 2
    rows_blocks = rows_in.reshape(sources // merged, merged * per_source, rows_in.shape[2])
    small_blocks = small_in.reshape(sources // merged, merged * per_source, small_in.shape[2])
    zeros_kv = jnp.zeros(key_rows.shape, jnp.float32)

    def advance(carry, pieces):
        query_part, key_add, value_add = block_terms(
            pieces[0], pieces[1], key_rows, value_rows, own_shard, groups
        )
        return ((carry[0] + key_add, carry[1] + value_add), query_part)

    (key_sum, value_sum), query_parts = lax.scan(
        advance, (zeros_kv, zeros_kv), (rows_blocks, small_blocks)
    )
    return (query_parts.reshape(sources, per_source, -1), key_sum, value_sum)


def general_local(query_rows, key_rows, value_rows, attn_out, out_grad, logsumexp, shard_pick, block_pick):
    head_size = query_rows.shape[1]
    q_count = query_rows.shape[0]
    scale = head_size ** (-0.5)
    out_local, grad_local = (
        lax.all_to_all(attn_out, "head", split_axis=1, concat_axis=0, tiled=True),
        lax.all_to_all(out_grad, "head", split_axis=1, concat_axis=0, tiled=True),
    )
    delta = jnp.sum(
        out_local.astype(jnp.float32) * grad_local.astype(jnp.float32), axis=1, keepdims=True
    ).astype(jnp.bfloat16)
    seq_count = lax.axis_size("seq")
    own_shard = lax.axis_index("seq")
    targets = shard_pick[0]
    groups = targets.shape[1]
    picks = block_pick[0].reshape(q_count, -1)
    row_data = jnp.concatenate([query_rows, grad_local], axis=1)
    small_data = jnp.concatenate(
        [
            logsumexp[0][:, None],
            delta,
            (targets + 1).astype(jnp.bfloat16),
            picks.astype(jnp.bfloat16),
        ],
        axis=1,
    )
    capacity = min(q_count, 2 * q_count * groups // seq_count)
    shard_ids = jnp.arange(seq_count, dtype=jnp.int32)
    hits = jnp.any(targets[:, :, None] == shard_ids[None, None, :], axis=1).astype(jnp.float32)
    row_ids = jnp.arange(q_count, dtype=jnp.int32)
    lower = (row_ids[:, None] >= row_ids[None, :]).astype(jnp.float32)
    slots = (
        jnp.dot(lower, hits, precision=lax.Precision.HIGHEST, preferred_element_type=jnp.float32)
        - 1.0
    )
    slot_ids = jnp.arange(capacity, dtype=jnp.float32)
    dispatch = hits.T[:, None, :] * (slots.T[:, None, :] == slot_ids[None, :, None]).astype(
        jnp.float32
    )
    dispatch_low = dispatch.astype(jnp.bfloat16)
    send_rows = jnp.einsum(
        "scr,rf->scf", dispatch_low, row_data, preferred_element_type=jnp.float32
    ).astype(jnp.bfloat16)
    send_small = jnp.einsum(
        "scr,rf->scf", dispatch_low, small_data, preferred_element_type=jnp.float32
    ).astype(jnp.bfloat16)
    got_rows, got_small = (
        lax.all_to_all(send_rows, "seq", split_axis=0, concat_axis=0, tiled=True),
        lax.all_to_all(send_small, "seq", split_axis=0, concat_axis=0, tiled=True),
    )
    query_parts, key_sum, value_sum = sweep(
        got_rows, got_small, key_rows, value_rows, own_shard, groups
    )
    returned = lax.all_to_all(query_parts, "seq", split_axis=0, concat_axis=0, tiled=True)
    total = jnp.einsum(
        "scr,scd->rd",
        dispatch,
        returned,
        precision=lax.Precision.HIGHEST,
        preferred_element_type=jnp.float32,
    )
    query_grad = (total * scale).astype(jnp.bfloat16)
    key_grad = (key_sum * scale).astype(jnp.bfloat16)
    value_grad = value_sum.astype(jnp.bfloat16)
    return (query_grad, key_grad, value_grad)


def swap(value, axis, count, bit):
    return lax.ppermute(value, axis, [(i, i ^ bit) for i in range(count)])


def row_sums(left, right):
    product = left.astype(jnp.float32) * right.astype(jnp.float32)
    high = product.astype(jnp.bfloat16)
    low = (product - high.astype(jnp.float32)).astype(jnp.bfloat16)
    ones = jnp.ones((8, product.shape[1]), jnp.bfloat16)
    contract = (((1,), (1,)), ((), ()))
    total = lax.dot_general(ones, high, contract, preferred_element_type=jnp.float32)
    total = total + lax.dot_general(ones, low, contract, preferred_element_type=jnp.float32)
    return total[0:1]


def unpack(parts, count):
    queries, grads, outs = (
        jnp.concatenate([r[k * count : (k + 1) * count] for r in parts], axis=0) for k in range(3)
    )
    small = [r[3 * count : 4 * count].astype(jnp.float32) for r in parts]
    lane = lax.broadcasted_iota(jnp.int32, small[0].shape, 1) // count
    merged = small[0]
    for k in range(1, len(parts)):
        merged = jnp.where(lane == k, small[k], merged)
    half = merged.shape[0] // 2
    delta = row_sums(outs, grads).astype(jnp.bfloat16).astype(jnp.float32)
    return queries, grads, delta, merged[0:1], merged[half:]


def chosen_offset(lse, ids, blocks, base):
    number = lax.broadcasted_iota(jnp.int32, (blocks, ids.shape[1]), 0) + base
    number = number.astype(jnp.float32)
    chosen = ids[0:1] == number
    for k in range(1, ids.shape[0]):
        chosen = chosen | (ids[k : k + 1] == number)
    return jnp.where(chosen, lse * LOG2E, 1e30)


def terms(queries, grads, delta, offset, keys, values, scale):
    contract = (((1,), (1,)), ((), ()))
    scores = lax.dot_general(keys, queries, contract, preferred_element_type=jnp.float32)
    dprob = lax.dot_general(values, grads, contract, preferred_element_type=jnp.float32)
    scores = scores.reshape(offset.shape[0], BLK, -1)
    probs = jnp.exp2(scores * (scale * LOG2E) - offset[:, None, :]).reshape(dprob.shape)
    return probs, probs * (dprob - delta)


def query_sums(scale, shard, bits, r0, r1, pairs):
    parts, count = (r0[...], r1[...]), r0.shape[0] // 4
    queries, grads, delta, lse, ids = unpack(parts + parts, count)
    half, size = 2 * count, queries.shape[1]
    row = lax.broadcasted_iota(jnp.int32, queries.shape, 0)
    lane = lax.broadcasted_iota(jnp.int32, (1, 2 * half), 1)

    def beside(value):
        zero = jnp.zeros_like(value)
        return jnp.concatenate(
            [jnp.where(row < half, value, zero), jnp.where(row < half, zero, value)], axis=1
        )

    queries, grads = beside(queries), beside(grads)
    wide, scored = [], []
    for (left_bit, right_bit), (left, right) in zip(bits, pairs):
        keys = jnp.concatenate([left[0], right[0]], axis=1)
        values = jnp.concatenate([left[1], right[1]], axis=1)
        blocks = keys.shape[0] // BLK
        base = jnp.where(lane < half, shard ^ left_bit, shard ^ right_bit) * blocks
        offset = chosen_offset(lse, ids, blocks, base)
        _, dscore = terms(queries, grads, delta, offset, keys, values, scale)
        wide.append(keys)
        scored.append(dscore.T.astype(jnp.bfloat16))
    scored, wide = jnp.concatenate(scored, axis=1), jnp.concatenate(wide, axis=0)
    total = jnp.dot(scored, wide, preferred_element_type=jnp.float32)
    return total[:half, :size] + total[half:, size:]


def near_kernel(scale, shard_ref, r0, r1, k0, v0, k1, v1, q_part):
    pair = ((k0[...], v0[...]), (k1[...], v1[...]))
    q_part[...] = query_sums(scale, shard_ref[0], ((0, 1),), r0, r1, (pair,))


def side_kernel(scale, shard_ref, r0, r1, q_part, k2, v2, k3, v3, q_own, q_out):
    count = r0.shape[0] // 4
    pair = ((k2[...], v2[...]), (k3[...], v3[...]))
    total = q_part[...] + query_sums(scale, shard_ref[0], ((2, 3),), r0, r1, (pair,))
    q_own[...] = total[:count]
    q_out[...] = total[count:].astype(q_out.dtype)


def key_sums(shard, parts, keys, values, scale):
    count = parts[0].shape[0] // 4
    queries, grads, delta, lse, ids = unpack(parts, count)
    blocks = keys.shape[0] // BLK
    offset = chosen_offset(lse, ids, blocks, shard * blocks)
    probs, dscore = terms(queries, grads, delta, offset, keys, values, scale)
    low = jnp.bfloat16
    v_sum = jnp.dot(probs.astype(low), grads, preferred_element_type=jnp.float32)
    k_sum = jnp.dot(dscore.astype(low), queries, preferred_element_type=jnp.float32)
    return k_sum, v_sum


def key_kernel(scale, shard_ref, lane, keys, values, k_part, v_part):
    parts = [lane[k] for k in range(lane.shape[0])]
    k_part[...], v_part[...] = key_sums(shard_ref[0], parts, keys[...], values[...], scale)


def query_sum_kernel(scale, q_own, q_back, q_sum):
    q_sum[...] = ((q_own[...] + q_back[...].astype(jnp.float32)) * scale).astype(q_sum.dtype)


def finish_kernel(
    scale, shard_ref, lane, keys, values, k_part, v_part, q_sum, q_out, k_out, v_out
):
    parts = [lane[k] for k in range(lane.shape[0])]
    k_sum, v_sum = key_sums(shard_ref[0], parts, keys[...], values[...], scale)
    k_out[...] = ((k_sum + k_part[...]) * scale).astype(k_out.dtype)
    v_out[...] = (v_sum + v_part[...]).astype(v_out.dtype)
    q_out[...] = q_sum[...]


def small_kernel(blocks_dev, queries, lse, shards, picks, early):
    count, size = queries.shape
    row = lax.broadcasted_iota(jnp.int32, (count, size), 0)
    lane = lax.broadcasted_iota(jnp.int32, (count, size), 1)
    repeat = (lane % count == row).astype(jnp.bfloat16)
    ids = [shards[g : g + 1] * blocks_dev + picks[g] for g in range(shards.shape[0])]
    ids = jnp.concatenate(ids, axis=0).astype(jnp.float32)
    stats = jnp.broadcast_to(lse[...].astype(jnp.float32), ids.shape)
    both = jnp.concatenate([stats, ids], axis=0).astype(jnp.bfloat16)
    early[:count] = queries[...]
    both = jnp.dot(both, repeat, preferred_element_type=jnp.float32)
    early[count:] = both.astype(early.dtype)


def fast_local(query_rows, key_rows, value_rows, attn_out, out_grad, logsumexp, shard_pick, block_pick):
    count, size = query_rows.shape
    kv = key_rows.shape
    n_seq, n_head = lax.axis_size("seq"), lax.axis_size("head")
    seq, head = lax.axis_index("seq"), lax.axis_index("head")
    scale = size ** (-0.5)
    f32, bf16 = jnp.float32, jnp.bfloat16
    vmem = pl.BlockSpec(memory_space=pltpu.VMEM)
    smem = pl.BlockSpec(memory_space=pltpu.SMEM)

    def kernel(body, name, outs, scalars, args, flops=None, last=False):
        cost = None
        if flops is not None:
            cost = pl.CostEstimate(
                flops=flops, bytes_accessed=max(flops // 1000, 1), transcendentals=0
            )
        return pl.pallas_call(
            body,
            out_shape=tuple(jax.ShapeDtypeStruct(v, t) for v, t in outs),
            in_specs=[smem] * len(scalars) + [vmem] * len(args),
            compiler_params=pltpu.CompilerParams(vmem_limit_bytes=32 * 1024 * 1024),
            cost_estimate=cost,
            name=name,
            **({} if last else dict(out_specs=(vmem,) * len(outs))),
        )(*(v[None].astype(jnp.int32) for v in scalars), *args)

    mine = jnp.stack([out_grad, attn_out])
    near = swap(mine, "head", n_head, 1)
    mine, keys, values = lax.optimization_barrier((mine, key_rows, value_rows))
    keys_side = swap(keys, "seq", n_seq, 2)
    values_side = swap(values, "seq", n_seq, 2)
    near, shard_pick, block_pick, query_rows, logsumexp = lax.optimization_barrier(
        (near, shard_pick, block_pick, query_rows, logsumexp)
    )

    def pieces(which):
        both = jnp.stack([mine, near], axis=1)
        return lax.dynamic_slice_in_dim(both, which * size, size, axis=3)

    here = pieces(head)
    other = swap(pieces(head ^ 2), "head", n_head, 2)
    near, keys, values = lax.optimization_barrier((near, key_rows, value_rows))
    keys_core = swap(keys, "seq", n_seq, 1)
    values_core = swap(values, "seq", n_seq, 1)
    keys_side_core = swap(keys_side, "seq", n_seq, 1)
    values_side_core = swap(values_side, "seq", n_seq, 1)
    (early,) = kernel(
        functools.partial(small_kernel, kv[0] // BLK), "small", [((2 * count, size), bf16)], (),
        (query_rows, logsumexp, shard_pick[0].T, block_pick[0].transpose(1, 2, 0)), flops=10**9,
    )
    early, other = lax.optimization_barrier((early, other))
    odd, high = (head & 1) == 1, (head & 2) == 2
    both = jnp.stack([jnp.where(high, other, here), jnp.where(high, here, other)], axis=1)
    both = jnp.where(odd, both[:, :, ::-1], both)
    both = both.reshape(2 * count, size)
    block = jnp.concatenate([early[:count], both, early[count:]], axis=0)
    block, keys_core, values_core = lax.optimization_barrier((block, keys_core, values_core))
    block_y = swap(block, "seq", n_seq, 4)
    block_x = swap(block, "seq", n_seq, 2)
    block_d = swap(block, "seq", n_seq, 6)
    (q_part,) = kernel(
        functools.partial(near_kernel, scale), "near_terms", [((2 * count, size), f32)], (seq,),
        (block, block_y, key_rows, value_rows, keys_core, values_core), flops=10**11,
    )
    q_own, q_out = kernel(
        functools.partial(side_kernel, scale), "side_terms",
        [((count, size), f32), ((count, size), bf16)], (seq,),
        (block, block_y, q_part, keys_side, values_side, keys_side_core, values_side_core),
    )
    _, block_x, block_d = lax.optimization_barrier((q_out, block_x, block_d))
    q_back = swap(q_out, "seq", n_seq, 4)
    lane = jnp.stack([block, block_y, block_x, block_d])
    lane_core = swap(lane, "seq", n_seq, 1)
    k_part, v_part = kernel(
        functools.partial(key_kernel, scale), "key_terms", [(kv, f32)] * 2, (seq,),
        (lane, key_rows, value_rows), flops=1,
    )
    (q_sum,) = kernel(
        functools.partial(query_sum_kernel, scale), "query_sum", [((count, size), bf16)], (),
        (q_own, q_back), flops=3 * 10**9,
    )
    return kernel(
        functools.partial(finish_kernel, scale), "finish",
        [((count, size), bf16), (kv, bf16), (kv, bf16)], (seq,),
        (lane_core, key_rows, value_rows, k_part, v_part, q_sum), last=True,
    )


def solution(mesh):
    placed = (
        P("seq", "head"),
        P("seq", "head"),
        P("seq", "head"),
        P(("seq", "head"), None),
        P(("seq", "head"), None),
        P("head", "seq"),
        P("head", "seq", None),
        P("head", "seq", None, None),
    )
    small = mesh.shape["seq"] == 8 and mesh.shape["head"] == 4

    def local(*args):
        count, size = args[0].shape
        fits = small and count * 4 == size == 128 and args[7].shape[2] * args[7].shape[3] == 16
        return (fast_local if fits else general_local)(*args)

    return jax.shard_map(
        local,
        mesh=mesh,
        in_specs=placed,
        out_specs=(P("seq", "head"), P("seq", "head"), P("seq", "head")),
        check_vma=False,
    )
```

```python
import functools

import jax
import jax.numpy as jnp
from jax import lax
from jax.experimental import pallas as pl
from jax.experimental.pallas import tpu as pltpu
from jax.sharding import PartitionSpec as P

BLK = 64
LOG2E = 1.4426950408889634


def block_terms(row_data, small_data, key_rows, value_rows, own_shard, groups):
    count = row_data.shape[0]
    head_size = key_rows.shape[1]
    per_shard = key_rows.shape[0] // BLK
    queries = row_data[:, :head_size]
    grads = row_data[:, head_size:]
    stats = small_data[:, :2].astype(jnp.float32)
    shards_of = small_data[:, 2 : 2 + groups].astype(jnp.int32)
    picks_of = small_data[:, 2 + groups :].astype(jnp.int32).reshape(count, groups, -1)
    local_ids = jnp.arange(per_shard, dtype=jnp.int32)
    matched = (shards_of == own_shard + 1)[:, :, None, None] & (
        picks_of[:, :, :, None] == local_ids[None, None, None, :]
    )
    chosen = jnp.any(matched, axis=(1, 2))
    mask = jnp.broadcast_to(chosen[:, :, None], (count, per_shard, BLK)).reshape(
        count, key_rows.shape[0]
    )
    scores = jnp.dot(queries, key_rows.T, preferred_element_type=jnp.float32) * head_size ** (-0.5)
    probs = jnp.where(mask, jnp.exp(scores - stats[:, 0:1]), 0.0)
    probs_low = probs.astype(jnp.bfloat16)
    value_add = jnp.dot(probs_low.T, grads, preferred_element_type=jnp.float32)
    dprob = jnp.dot(grads, value_rows.T, preferred_element_type=jnp.float32)
    dscore = (probs * (dprob - stats[:, 1:2])).astype(jnp.bfloat16)
    key_add = jnp.dot(dscore.T, queries, preferred_element_type=jnp.float32)
    query_part = jnp.dot(dscore, key_rows, preferred_element_type=jnp.float32)
    return (query_part, key_add, value_add)


def sweep(rows_in, small_in, key_rows, value_rows, own_shard, groups):
    sources, per_source = (rows_in.shape[0], rows_in.shape[1])
    merged = 1
    while merged * 2 <= sources and sources % (merged * 2) == 0 and (merged * per_source < 512):
        merged = merged * 2
    rows_blocks = rows_in.reshape(sources // merged, merged * per_source, rows_in.shape[2])
    small_blocks = small_in.reshape(sources // merged, merged * per_source, small_in.shape[2])
    zeros_kv = jnp.zeros(key_rows.shape, jnp.float32)

    def advance(carry, pieces):
        query_part, key_add, value_add = block_terms(
            pieces[0], pieces[1], key_rows, value_rows, own_shard, groups
        )
        return ((carry[0] + key_add, carry[1] + value_add), query_part)

    (key_sum, value_sum), query_parts = lax.scan(
        advance, (zeros_kv, zeros_kv), (rows_blocks, small_blocks)
    )
    return (query_parts.reshape(sources, per_source, -1), key_sum, value_sum)


def general_local(query_rows, key_rows, value_rows, attn_out, out_grad, logsumexp, shard_pick, block_pick):
    head_size = query_rows.shape[1]
    q_count = query_rows.shape[0]
    scale = head_size ** (-0.5)
    out_local, grad_local = (
        lax.all_to_all(attn_out, "head", split_axis=1, concat_axis=0, tiled=True),
        lax.all_to_all(out_grad, "head", split_axis=1, concat_axis=0, tiled=True),
    )
    delta = jnp.sum(
        out_local.astype(jnp.float32) * grad_local.astype(jnp.float32), axis=1, keepdims=True
    ).astype(jnp.bfloat16)
    seq_count = lax.axis_size("seq")
    own_shard = lax.axis_index("seq")
    targets = shard_pick[0]
    groups = targets.shape[1]
    picks = block_pick[0].reshape(q_count, -1)
    row_data = jnp.concatenate([query_rows, grad_local], axis=1)
    small_data = jnp.concatenate(
        [
            logsumexp[0][:, None],
            delta,
            (targets + 1).astype(jnp.bfloat16),
            picks.astype(jnp.bfloat16),
        ],
        axis=1,
    )
    capacity = min(q_count, 2 * q_count * groups // seq_count)
    shard_ids = jnp.arange(seq_count, dtype=jnp.int32)
    hits = jnp.any(targets[:, :, None] == shard_ids[None, None, :], axis=1).astype(jnp.float32)
    row_ids = jnp.arange(q_count, dtype=jnp.int32)
    lower = (row_ids[:, None] >= row_ids[None, :]).astype(jnp.float32)
    slots = (
        jnp.dot(lower, hits, precision=lax.Precision.HIGHEST, preferred_element_type=jnp.float32)
        - 1.0
    )
    slot_ids = jnp.arange(capacity, dtype=jnp.float32)
    dispatch = hits.T[:, None, :] * (slots.T[:, None, :] == slot_ids[None, :, None]).astype(
        jnp.float32
    )
    dispatch_low = dispatch.astype(jnp.bfloat16)
    send_rows = jnp.einsum(
        "scr,rf->scf", dispatch_low, row_data, preferred_element_type=jnp.float32
    ).astype(jnp.bfloat16)
    send_small = jnp.einsum(
        "scr,rf->scf", dispatch_low, small_data, preferred_element_type=jnp.float32
    ).astype(jnp.bfloat16)
    got_rows, got_small = (
        lax.all_to_all(send_rows, "seq", split_axis=0, concat_axis=0, tiled=True),
        lax.all_to_all(send_small, "seq", split_axis=0, concat_axis=0, tiled=True),
    )
    query_parts, key_sum, value_sum = sweep(
        got_rows, got_small, key_rows, value_rows, own_shard, groups
    )
    returned = lax.all_to_all(query_parts, "seq", split_axis=0, concat_axis=0, tiled=True)
    total = jnp.einsum(
        "scr,scd->rd",
        dispatch,
        returned,
        precision=lax.Precision.HIGHEST,
        preferred_element_type=jnp.float32,
    )
    query_grad = (total * scale).astype(jnp.bfloat16)
    key_grad = (key_sum * scale).astype(jnp.bfloat16)
    value_grad = value_sum.astype(jnp.bfloat16)
    return (query_grad, key_grad, value_grad)


def swap(value, axis, count, bit):
    return lax.ppermute(value, axis, [(i, i ^ bit) for i in range(count)])


def row_sums(left, right):
    product = left.astype(jnp.float32) * right.astype(jnp.float32)
    high = product.astype(jnp.bfloat16)
    low = (product - high.astype(jnp.float32)).astype(jnp.bfloat16)
    ones = jnp.ones((8, product.shape[1]), jnp.bfloat16)
    contract = (((1,), (1,)), ((), ()))
    total = lax.dot_general(ones, high, contract, preferred_element_type=jnp.float32)
    total = total + lax.dot_general(ones, low, contract, preferred_element_type=jnp.float32)
    return total[0:1]


def unpack(parts, count):
    queries, grads, outs = (
        jnp.concatenate([r[k * count : (k + 1) * count] for r in parts], axis=0) for k in range(3)
    )
    small = [r[3 * count : 4 * count].astype(jnp.float32) for r in parts]
    lane = lax.broadcasted_iota(jnp.int32, small[0].shape, 1) // count
    merged = small[0]
    for k in range(1, len(parts)):
        merged = jnp.where(lane == k, small[k], merged)
    half = merged.shape[0] // 2
    delta = row_sums(outs, grads).astype(jnp.bfloat16).astype(jnp.float32)
    return queries, grads, delta, merged[0:1], merged[half:]


def chosen_offset(lse, ids, blocks, base):
    number = lax.broadcasted_iota(jnp.int32, (blocks, ids.shape[1]), 0) + base
    number = number.astype(jnp.float32)
    chosen = ids[0:1] == number
    for k in range(1, ids.shape[0]):
        chosen = chosen | (ids[k : k + 1] == number)
    return jnp.where(chosen, lse * LOG2E, 1e30)


def terms(queries, grads, delta, offset, keys, values, scale):
    contract = (((1,), (1,)), ((), ()))
    scores = lax.dot_general(keys, queries, contract, preferred_element_type=jnp.float32)
    dprob = lax.dot_general(values, grads, contract, preferred_element_type=jnp.float32)
    scores = scores.reshape(offset.shape[0], BLK, -1)
    probs = jnp.exp2(scores * (scale * LOG2E) - offset[:, None, :]).reshape(dprob.shape)
    return probs, probs * (dprob - delta)


def doubled(r0, r1):
    parts, count = (r0[...], r1[...]), r0.shape[0] // 4
    queries, grads, delta, lse, ids = unpack(parts + parts, count)
    row = lax.broadcasted_iota(jnp.int32, queries.shape, 0)

    def beside(value):
        zero = jnp.zeros_like(value)
        return jnp.concatenate(
            [jnp.where(row < 2 * count, value, zero), jnp.where(row < 2 * count, zero, value)], axis=1
        )

    return beside(queries), beside(grads), delta, lse, ids


def rows_kernel(r0, r1, queries, grads, stats):
    queries[...], grads[...], delta, lse, ids = doubled(r0, r1)
    stats[0:1], stats[1:2], stats[8:] = delta, lse, ids


def query_kernel(
    scale, shard_ref, queries, grads, stats, k0, v0, k1, v1, k2, v2, k3, v3, q_own, q_out
):
    half, size, count = queries.shape[0] // 2, queries.shape[1] // 2, q_own.shape[0]
    delta, lse, ids = stats[0:1], stats[1:2], stats[8:]
    lane = lax.broadcasted_iota(jnp.int32, (1, 2 * half), 1)
    wide, scored = [], []
    for bit, left, right in ((0, (k0, v0), (k1, v1)), (2, (k2, v2), (k3, v3))):
        keys = jnp.concatenate([left[0][...], right[0][...]], axis=1)
        values = jnp.concatenate([left[1][...], right[1][...]], axis=1)
        blocks = keys.shape[0] // BLK
        base = jnp.where(lane < half, shard_ref[0] ^ bit, shard_ref[0] ^ (bit + 1)) * blocks
        offset = chosen_offset(lse, ids, blocks, base)
        _, dscore = terms(queries[...], grads[...], delta, offset, keys, values, scale)
        wide.append(keys)
        scored.append(dscore.T.astype(jnp.bfloat16))
    scored, wide = jnp.concatenate(scored, axis=1), jnp.concatenate(wide, axis=0)
    total = jnp.dot(scored, wide, preferred_element_type=jnp.float32)
    total = total[:half, :size] + total[half:, size:]
    q_own[...] = total[:count]
    q_out[...] = total[count:].astype(q_out.dtype)


def key_sums(shard, parts, keys, values, scale):
    count = parts[0].shape[0] // 4
    queries, grads, delta, lse, ids = unpack(parts, count)
    blocks = keys.shape[0] // BLK
    offset = chosen_offset(lse, ids, blocks, shard * blocks)
    probs, dscore = terms(queries, grads, delta, offset, keys, values, scale)
    low = jnp.bfloat16
    v_sum = jnp.dot(probs.astype(low), grads, preferred_element_type=jnp.float32)
    k_sum = jnp.dot(dscore.astype(low), queries, preferred_element_type=jnp.float32)
    return k_sum, v_sum


def key_kernel(scale, shard_ref, lane, keys, values, k_part, v_part):
    parts = [lane[k] for k in range(lane.shape[0])]
    k_part[...], v_part[...] = key_sums(shard_ref[0], parts, keys[...], values[...], scale)


def query_sum_kernel(scale, q_own, q_back, q_sum):
    q_sum[...] = ((q_own[...] + q_back[...].astype(jnp.float32)) * scale).astype(q_sum.dtype)


def finish_kernel(
    scale, shard_ref, lane, keys, values, k_part, v_part, q_sum, q_out, k_out, v_out
):
    parts = [lane[k] for k in range(lane.shape[0])]
    k_sum, v_sum = key_sums(shard_ref[0], parts, keys[...], values[...], scale)
    k_out[...] = ((k_sum + k_part[...]) * scale).astype(k_out.dtype)
    v_out[...] = (v_sum + v_part[...]).astype(v_out.dtype)
    q_out[...] = q_sum[...]


def small_kernel(blocks_dev, queries, lse, shards, picks, early):
    count, size = queries.shape
    row = lax.broadcasted_iota(jnp.int32, (count, size), 0)
    lane = lax.broadcasted_iota(jnp.int32, (count, size), 1)
    repeat = (lane % count == row).astype(jnp.bfloat16)
    ids = [shards[g : g + 1] * blocks_dev + picks[g] for g in range(shards.shape[0])]
    ids = jnp.concatenate(ids, axis=0).astype(jnp.float32)
    stats = jnp.broadcast_to(lse[...].astype(jnp.float32), ids.shape)
    both = jnp.concatenate([stats, ids], axis=0).astype(jnp.bfloat16)
    early[:count] = queries[...]
    both = jnp.dot(both, repeat, preferred_element_type=jnp.float32)
    early[count:] = both.astype(early.dtype)


def fast_local(query_rows, key_rows, value_rows, attn_out, out_grad, logsumexp, shard_pick, block_pick):
    count, size = query_rows.shape
    kv = key_rows.shape
    n_seq, n_head = lax.axis_size("seq"), lax.axis_size("head")
    seq, head = lax.axis_index("seq"), lax.axis_index("head")
    scale = size ** (-0.5)
    f32, bf16 = jnp.float32, jnp.bfloat16
    vmem = pl.BlockSpec(memory_space=pltpu.VMEM)
    smem = pl.BlockSpec(memory_space=pltpu.SMEM)

    def kernel(body, name, outs, scalars, args, flops=None, last=False):
        cost = None
        if flops is not None:
            cost = pl.CostEstimate(
                flops=flops, bytes_accessed=max(flops // 1000, 1), transcendentals=0
            )
        return pl.pallas_call(
            body,
            out_shape=tuple(jax.ShapeDtypeStruct(v, t) for v, t in outs),
            in_specs=[smem] * len(scalars) + [vmem] * len(args),
            compiler_params=pltpu.CompilerParams(vmem_limit_bytes=32 * 1024 * 1024),
            cost_estimate=cost,
            name=name,
            **({} if last else dict(out_specs=(vmem,) * len(outs))),
        )(*(v[None].astype(jnp.int32) for v in scalars), *args)

    mine = jnp.stack([out_grad, attn_out])
    near = swap(mine, "head", n_head, 1)
    mine, keys, values = lax.optimization_barrier((mine, key_rows, value_rows))
    keys_side = swap(keys, "seq", n_seq, 2)
    values_side = swap(values, "seq", n_seq, 2)
    near, shard_pick, block_pick, query_rows, logsumexp = lax.optimization_barrier(
        (near, shard_pick, block_pick, query_rows, logsumexp)
    )

    def pieces(which):
        both = jnp.stack([mine, near], axis=1)
        return lax.dynamic_slice_in_dim(both, which * size, size, axis=3)

    here = pieces(head)
    other = swap(pieces(head ^ 2), "head", n_head, 2)
    near, keys, values = lax.optimization_barrier((near, key_rows, value_rows))
    keys_core = swap(keys, "seq", n_seq, 1)
    values_core = swap(values, "seq", n_seq, 1)
    keys_side_core = swap(keys_side, "seq", n_seq, 1)
    values_side_core = swap(values_side, "seq", n_seq, 1)
    (early,) = kernel(
        functools.partial(small_kernel, kv[0] // BLK), "small", [((2 * count, size), bf16)], (),
        (query_rows, logsumexp, shard_pick[0].T, block_pick[0].transpose(1, 2, 0)), flops=10**9,
    )
    early, other = lax.optimization_barrier((early, other))
    odd, high = (head & 1) == 1, (head & 2) == 2
    both = jnp.stack([jnp.where(high, other, here), jnp.where(high, here, other)], axis=1)
    both = jnp.where(odd, both[:, :, ::-1], both)
    both = both.reshape(2 * count, size)
    block = jnp.concatenate([early[:count], both, early[count:]], axis=0)
    block, keys_core, values_core = lax.optimization_barrier((block, keys_core, values_core))
    block_y = swap(block, "seq", n_seq, 4)
    block_x = swap(block, "seq", n_seq, 2)
    block_d = swap(block, "seq", n_seq, 6)
    wide = (4 * count, 2 * size)
    rows = kernel(
        rows_kernel, "rows", [(wide, bf16), (wide, bf16), ((24, 4 * count), f32)], (),
        (block, block_y), flops=10**11,
    )
    q_own, q_out = kernel(
        functools.partial(query_kernel, scale), "query_terms",
        [((count, size), f32), ((count, size), bf16)], (seq,),
        (*rows, key_rows, value_rows, keys_core, values_core)
        + (keys_side, values_side, keys_side_core, values_side_core),
        flops=1,
    )
    _, block_x, block_d = lax.optimization_barrier((q_out, block_x, block_d))
    q_back = swap(q_out, "seq", n_seq, 4)
    lane = jnp.stack([block, block_y, block_x, block_d])
    lane_core = swap(lane, "seq", n_seq, 1)
    k_part, v_part = kernel(
        functools.partial(key_kernel, scale), "key_terms", [(kv, f32)] * 2, (seq,),
        (lane, key_rows, value_rows), flops=3 * 10**9,
    )
    (q_sum,) = kernel(
        functools.partial(query_sum_kernel, scale), "query_sum", [((count, size), bf16)], (),
        (q_own, q_back), flops=10**9,
    )
    return kernel(
        functools.partial(finish_kernel, scale), "finish",
        [((count, size), bf16), (kv, bf16), (kv, bf16)], (seq,),
        (lane_core, key_rows, value_rows, k_part, v_part, q_sum), last=True,
    )


def solution(mesh):
    placed = (
        P("seq", "head"),
        P("seq", "head"),
        P("seq", "head"),
        P(("seq", "head"), None),
        P(("seq", "head"), None),
        P("head", "seq"),
        P("head", "seq", None),
        P("head", "seq", None, None),
    )
    small = mesh.shape["seq"] == 8 and mesh.shape["head"] == 4

    def local(*args):
        count, size = args[0].shape
        fits = small and count * 4 == size == 128 and args[7].shape[2] * args[7].shape[3] == 16
        return (fast_local if fits else general_local)(*args)

    return jax.shard_map(
        local,
        mesh=mesh,
        in_specs=placed,
        out_specs=(P("seq", "head"), P("seq", "head"), P("seq", "head")),
        check_vma=False,
    )
```

```python
import functools

import jax
import jax.numpy as jnp
from jax import lax
from jax.experimental import pallas as pl
from jax.experimental.pallas import tpu as pltpu
from jax.sharding import PartitionSpec as P

BLK = 64
LOG2E = 1.4426950408889634


def block_terms(row_data, small_data, key_rows, value_rows, own_shard, groups):
    count = row_data.shape[0]
    head_size = key_rows.shape[1]
    per_shard = key_rows.shape[0] // BLK
    queries = row_data[:, :head_size]
    grads = row_data[:, head_size:]
    stats = small_data[:, :2].astype(jnp.float32)
    shards_of = small_data[:, 2 : 2 + groups].astype(jnp.int32)
    picks_of = small_data[:, 2 + groups :].astype(jnp.int32).reshape(count, groups, -1)
    local_ids = jnp.arange(per_shard, dtype=jnp.int32)
    matched = (shards_of == own_shard + 1)[:, :, None, None] & (
        picks_of[:, :, :, None] == local_ids[None, None, None, :]
    )
    chosen = jnp.any(matched, axis=(1, 2))
    mask = jnp.broadcast_to(chosen[:, :, None], (count, per_shard, BLK)).reshape(
        count, key_rows.shape[0]
    )
    scores = jnp.dot(queries, key_rows.T, preferred_element_type=jnp.float32) * head_size ** (-0.5)
    probs = jnp.where(mask, jnp.exp(scores - stats[:, 0:1]), 0.0)
    probs_low = probs.astype(jnp.bfloat16)
    value_add = jnp.dot(probs_low.T, grads, preferred_element_type=jnp.float32)
    dprob = jnp.dot(grads, value_rows.T, preferred_element_type=jnp.float32)
    dscore = (probs * (dprob - stats[:, 1:2])).astype(jnp.bfloat16)
    key_add = jnp.dot(dscore.T, queries, preferred_element_type=jnp.float32)
    query_part = jnp.dot(dscore, key_rows, preferred_element_type=jnp.float32)
    return (query_part, key_add, value_add)


def sweep(rows_in, small_in, key_rows, value_rows, own_shard, groups):
    sources, per_source = (rows_in.shape[0], rows_in.shape[1])
    merged = 1
    while merged * 2 <= sources and sources % (merged * 2) == 0 and (merged * per_source < 512):
        merged = merged * 2
    rows_blocks = rows_in.reshape(sources // merged, merged * per_source, rows_in.shape[2])
    small_blocks = small_in.reshape(sources // merged, merged * per_source, small_in.shape[2])
    zeros_kv = jnp.zeros(key_rows.shape, jnp.float32)

    def advance(carry, pieces):
        query_part, key_add, value_add = block_terms(
            pieces[0], pieces[1], key_rows, value_rows, own_shard, groups
        )
        return ((carry[0] + key_add, carry[1] + value_add), query_part)

    (key_sum, value_sum), query_parts = lax.scan(
        advance, (zeros_kv, zeros_kv), (rows_blocks, small_blocks)
    )
    return (query_parts.reshape(sources, per_source, -1), key_sum, value_sum)


def general_local(query_rows, key_rows, value_rows, attn_out, out_grad, logsumexp, shard_pick, block_pick):
    head_size = query_rows.shape[1]
    q_count = query_rows.shape[0]
    scale = head_size ** (-0.5)
    out_local, grad_local = (
        lax.all_to_all(attn_out, "head", split_axis=1, concat_axis=0, tiled=True),
        lax.all_to_all(out_grad, "head", split_axis=1, concat_axis=0, tiled=True),
    )
    delta = jnp.sum(
        out_local.astype(jnp.float32) * grad_local.astype(jnp.float32), axis=1, keepdims=True
    ).astype(jnp.bfloat16)
    seq_count = lax.axis_size("seq")
    own_shard = lax.axis_index("seq")
    targets = shard_pick[0]
    groups = targets.shape[1]
    picks = block_pick[0].reshape(q_count, -1)
    row_data = jnp.concatenate([query_rows, grad_local], axis=1)
    small_data = jnp.concatenate(
        [
            logsumexp[0][:, None],
            delta,
            (targets + 1).astype(jnp.bfloat16),
            picks.astype(jnp.bfloat16),
        ],
        axis=1,
    )
    capacity = min(q_count, 2 * q_count * groups // seq_count)
    shard_ids = jnp.arange(seq_count, dtype=jnp.int32)
    hits = jnp.any(targets[:, :, None] == shard_ids[None, None, :], axis=1).astype(jnp.float32)
    row_ids = jnp.arange(q_count, dtype=jnp.int32)
    lower = (row_ids[:, None] >= row_ids[None, :]).astype(jnp.float32)
    slots = (
        jnp.dot(lower, hits, precision=lax.Precision.HIGHEST, preferred_element_type=jnp.float32)
        - 1.0
    )
    slot_ids = jnp.arange(capacity, dtype=jnp.float32)
    dispatch = hits.T[:, None, :] * (slots.T[:, None, :] == slot_ids[None, :, None]).astype(
        jnp.float32
    )
    dispatch_low = dispatch.astype(jnp.bfloat16)
    send_rows = jnp.einsum(
        "scr,rf->scf", dispatch_low, row_data, preferred_element_type=jnp.float32
    ).astype(jnp.bfloat16)
    send_small = jnp.einsum(
        "scr,rf->scf", dispatch_low, small_data, preferred_element_type=jnp.float32
    ).astype(jnp.bfloat16)
    got_rows, got_small = (
        lax.all_to_all(send_rows, "seq", split_axis=0, concat_axis=0, tiled=True),
        lax.all_to_all(send_small, "seq", split_axis=0, concat_axis=0, tiled=True),
    )
    query_parts, key_sum, value_sum = sweep(
        got_rows, got_small, key_rows, value_rows, own_shard, groups
    )
    returned = lax.all_to_all(query_parts, "seq", split_axis=0, concat_axis=0, tiled=True)
    total = jnp.einsum(
        "scr,scd->rd",
        dispatch,
        returned,
        precision=lax.Precision.HIGHEST,
        preferred_element_type=jnp.float32,
    )
    query_grad = (total * scale).astype(jnp.bfloat16)
    key_grad = (key_sum * scale).astype(jnp.bfloat16)
    value_grad = value_sum.astype(jnp.bfloat16)
    return (query_grad, key_grad, value_grad)


def swap(value, axis, count, bit):
    return lax.ppermute(value, axis, [(i, i ^ bit) for i in range(count)])


def row_sums(left, right):
    product = left.astype(jnp.float32) * right.astype(jnp.float32)
    high = product.astype(jnp.bfloat16)
    low = (product - high.astype(jnp.float32)).astype(jnp.bfloat16)
    both = jnp.concatenate([high, low], axis=1)
    ones = jnp.ones((8, both.shape[1]), jnp.bfloat16)
    contract = (((1,), (1,)), ((), ()))
    return lax.dot_general(ones, both, contract, preferred_element_type=jnp.float32)[0:1]


def unpack(parts, count):
    queries, grads, outs = (
        jnp.concatenate([r[k * count : (k + 1) * count] for r in parts], axis=0) for k in range(3)
    )
    small = [r[3 * count : 4 * count].astype(jnp.float32) for r in parts]
    lane = lax.broadcasted_iota(jnp.int32, small[0].shape, 1) // count
    merged = small[0]
    for k in range(1, len(parts)):
        merged = jnp.where(lane == k, small[k], merged)
    half = merged.shape[0] // 2
    delta = row_sums(outs, grads).astype(jnp.bfloat16).astype(jnp.float32)
    return queries, grads, delta, merged[0:1], merged[half:]


def chosen_offset(lse, ids, blocks, base):
    number = lax.broadcasted_iota(jnp.int32, (blocks, ids.shape[1]), 0) + base
    number = number.astype(jnp.float32)
    chosen = ids[0:1] == number
    for k in range(1, ids.shape[0]):
        chosen = chosen | (ids[k : k + 1] == number)
    return jnp.where(chosen, lse * LOG2E, 1e30)


def terms(queries, grads, delta, offset, keys, values, scale):
    contract = (((1,), (1,)), ((), ()))
    scores = lax.dot_general(keys, queries, contract, preferred_element_type=jnp.float32)
    dprob = lax.dot_general(values, grads, contract, preferred_element_type=jnp.float32)
    scores = scores.reshape(offset.shape[0], BLK, -1)
    probs = jnp.exp2(scores * (scale * LOG2E) - offset[:, None, :]).reshape(dprob.shape)
    return probs, probs * (dprob - delta)


def doubled(r0, r1):
    parts, count = (r0[...], r1[...]), r0.shape[0] // 4
    queries, grads, delta, lse, ids = unpack(parts + parts, count)
    row = lax.broadcasted_iota(jnp.int32, queries.shape, 0)

    def beside(value):
        zero = jnp.zeros_like(value)
        return jnp.concatenate(
            [jnp.where(row < 2 * count, value, zero), jnp.where(row < 2 * count, zero, value)], axis=1
        )

    return beside(queries), beside(grads), delta, lse, ids


def rows_kernel(r0, r1, queries, grads, stats):
    queries[...], grads[...], delta, lse, ids = doubled(r0, r1)
    stats[0:1], stats[1:2], stats[8:] = delta, lse, ids


def query_kernel(
    scale, shard_ref, queries, grads, stats, k0, v0, k1, v1, k2, v2, k3, v3, q_own, q_out
):
    half, size, count = queries.shape[0] // 2, queries.shape[1] // 2, q_own.shape[0]
    delta, lse, ids = stats[0:1], stats[1:2], stats[8:]
    lane = lax.broadcasted_iota(jnp.int32, (1, 2 * half), 1)
    wide, scored = [], []
    for bit, left, right in ((0, (k0, v0), (k1, v1)), (2, (k2, v2), (k3, v3))):
        keys = jnp.concatenate([left[0][...], right[0][...]], axis=1)
        values = jnp.concatenate([left[1][...], right[1][...]], axis=1)
        blocks = keys.shape[0] // BLK
        base = jnp.where(lane < half, shard_ref[0] ^ bit, shard_ref[0] ^ (bit + 1)) * blocks
        offset = chosen_offset(lse, ids, blocks, base)
        _, dscore = terms(queries[...], grads[...], delta, offset, keys, values, scale)
        wide.append(keys)
        scored.append(dscore.T.astype(jnp.bfloat16))
    scored, wide = jnp.concatenate(scored, axis=1), jnp.concatenate(wide, axis=0)
    total = jnp.dot(scored, wide, preferred_element_type=jnp.float32)
    total = total[:half, :size] + total[half:, size:]
    q_own[...] = total[:count]
    q_out[...] = total[count:].astype(q_out.dtype)


def key_sums(shard, parts, keys, values, scale):
    count = parts[0].shape[0] // 4
    queries, grads, delta, lse, ids = unpack(parts, count)
    blocks = keys.shape[0] // BLK
    offset = chosen_offset(lse, ids, blocks, shard * blocks)
    probs, dscore = terms(queries, grads, delta, offset, keys, values, scale)
    low = jnp.bfloat16
    v_sum = jnp.dot(probs.astype(low), grads, preferred_element_type=jnp.float32)
    k_sum = jnp.dot(dscore.astype(low), queries, preferred_element_type=jnp.float32)
    return k_sum, v_sum


def key_kernel(scale, shard_ref, lane, keys, values, k_part, v_part):
    parts = [lane[k] for k in range(lane.shape[0])]
    k_part[...], v_part[...] = key_sums(shard_ref[0], parts, keys[...], values[...], scale)


def query_sum_kernel(scale, q_own, q_back, q_sum):
    q_sum[...] = ((q_own[...] + q_back[...].astype(jnp.float32)) * scale).astype(q_sum.dtype)


def finish_kernel(
    scale, shard_ref, lane, keys, values, k_part, v_part, q_sum, q_out, k_out, v_out
):
    parts = [lane[k] for k in range(lane.shape[0])]
    k_sum, v_sum = key_sums(shard_ref[0], parts, keys[...], values[...], scale)
    k_out[...] = ((k_sum + k_part[...]) * scale).astype(k_out.dtype)
    v_out[...] = (v_sum + v_part[...]).astype(v_out.dtype)
    q_out[...] = q_sum[...]


def small_kernel(blocks_dev, queries, lse, shards, picks, early):
    count, size = queries.shape
    row = lax.broadcasted_iota(jnp.int32, (count, size), 0)
    lane = lax.broadcasted_iota(jnp.int32, (count, size), 1)
    repeat = (lane % count == row).astype(jnp.bfloat16)
    ids = [shards[g : g + 1] * blocks_dev + picks[g] for g in range(shards.shape[0])]
    ids = jnp.concatenate(ids, axis=0).astype(jnp.float32)
    stats = jnp.broadcast_to(lse[...].astype(jnp.float32), ids.shape)
    both = jnp.concatenate([stats, ids], axis=0).astype(jnp.bfloat16)
    early[:count] = queries[...]
    both = jnp.dot(both, repeat, preferred_element_type=jnp.float32)
    early[count:] = both.astype(early.dtype)


def fast_local(query_rows, key_rows, value_rows, attn_out, out_grad, logsumexp, shard_pick, block_pick):
    count, size = query_rows.shape
    kv = key_rows.shape
    n_seq, n_head = lax.axis_size("seq"), lax.axis_size("head")
    seq, head = lax.axis_index("seq"), lax.axis_index("head")
    scale = size ** (-0.5)
    f32, bf16 = jnp.float32, jnp.bfloat16
    vmem = pl.BlockSpec(memory_space=pltpu.VMEM)
    smem = pl.BlockSpec(memory_space=pltpu.SMEM)

    def kernel(body, name, outs, scalars, args, flops=None, last=False):
        cost = None
        if flops is not None:
            cost = pl.CostEstimate(
                flops=flops, bytes_accessed=max(flops // 1000, 1), transcendentals=0
            )
        return pl.pallas_call(
            body,
            out_shape=tuple(jax.ShapeDtypeStruct(v, t) for v, t in outs),
            in_specs=[smem] * len(scalars) + [vmem] * len(args),
            compiler_params=pltpu.CompilerParams(vmem_limit_bytes=32 * 1024 * 1024),
            cost_estimate=cost,
            name=name,
            **({} if last else dict(out_specs=(vmem,) * len(outs))),
        )(*(v[None].astype(jnp.int32) for v in scalars), *args)

    mine = jnp.stack([out_grad, attn_out])
    near = swap(mine, "head", n_head, 1)
    mine, keys, values = lax.optimization_barrier((mine, key_rows, value_rows))
    keys_side = swap(keys, "seq", n_seq, 2)
    values_side = swap(values, "seq", n_seq, 2)
    near, shard_pick, block_pick, query_rows, logsumexp = lax.optimization_barrier(
        (near, shard_pick, block_pick, query_rows, logsumexp)
    )

    def pieces(which):
        both = jnp.stack([mine, near], axis=1)
        return lax.dynamic_slice_in_dim(both, which * size, size, axis=3)

    here = pieces(head)
    other = swap(pieces(head ^ 2), "head", n_head, 2)
    near, keys, values = lax.optimization_barrier((near, key_rows, value_rows))
    keys_core = swap(keys, "seq", n_seq, 1)
    values_core = swap(values, "seq", n_seq, 1)
    keys_side_core = swap(keys_side, "seq", n_seq, 1)
    values_side_core = swap(values_side, "seq", n_seq, 1)
    (early,) = kernel(
        functools.partial(small_kernel, kv[0] // BLK), "small", [((2 * count, size), bf16)], (),
        (query_rows, logsumexp, shard_pick[0].T, block_pick[0].transpose(1, 2, 0)), flops=10**9,
    )
    early, other = lax.optimization_barrier((early, other))
    odd, high = (head & 1) == 1, (head & 2) == 2
    both = jnp.stack([jnp.where(high, other, here), jnp.where(high, here, other)], axis=1)
    both = jnp.where(odd, both[:, :, ::-1], both)
    both = both.reshape(2 * count, size)
    block = jnp.concatenate([early[:count], both, early[count:]], axis=0)
    block, keys_core, values_core = lax.optimization_barrier((block, keys_core, values_core))
    block_y = swap(block, "seq", n_seq, 4)
    block_x = swap(block, "seq", n_seq, 2)
    block_d = swap(block, "seq", n_seq, 6)
    wide = (4 * count, 2 * size)
    rows = kernel(
        rows_kernel, "rows", [(wide, bf16), (wide, bf16), ((24, 4 * count), f32)], (),
        (block, block_y), flops=10**11,
    )
    q_own, q_out = kernel(
        functools.partial(query_kernel, scale), "query_terms",
        [((count, size), f32), ((count, size), bf16)], (seq,),
        (*rows, key_rows, value_rows, keys_core, values_core)
        + (keys_side, values_side, keys_side_core, values_side_core),
        flops=1,
    )
    _, block_x, block_d = lax.optimization_barrier((q_out, block_x, block_d))
    q_back = swap(q_out, "seq", n_seq, 4)
    lane = jnp.stack([block, block_y, block_x, block_d])
    lane_core = swap(lane, "seq", n_seq, 1)
    k_part, v_part = kernel(
        functools.partial(key_kernel, scale), "key_terms", [(kv, f32)] * 2, (seq,),
        (lane, key_rows, value_rows), flops=3 * 10**9,
    )
    (q_sum,) = kernel(
        functools.partial(query_sum_kernel, scale), "query_sum", [((count, size), bf16)], (),
        (q_own, q_back), flops=10**9,
    )
    return kernel(
        functools.partial(finish_kernel, scale), "finish",
        [((count, size), bf16), (kv, bf16), (kv, bf16)], (seq,),
        (lane_core, key_rows, value_rows, k_part, v_part, q_sum), last=True,
    )


def solution(mesh):
    placed = (
        P("seq", "head"),
        P("seq", "head"),
        P("seq", "head"),
        P(("seq", "head"), None),
        P(("seq", "head"), None),
        P("head", "seq"),
        P("head", "seq", None),
        P("head", "seq", None, None),
    )
    small = mesh.shape["seq"] == 8 and mesh.shape["head"] == 4

    def local(*args):
        count, size = args[0].shape
        fits = small and count * 4 == size == 128 and args[7].shape[2] * args[7].shape[3] == 16
        return (fast_local if fits else general_local)(*args)

    return jax.shard_map(
        local,
        mesh=mesh,
        in_specs=placed,
        out_specs=(P("seq", "head"), P("seq", "head"), P("seq", "head")),
        check_vma=False,
    )
```

```python
import functools

import jax
import jax.numpy as jnp
from jax import lax
from jax.experimental import pallas as pl
from jax.experimental.pallas import tpu as pltpu
from jax.sharding import PartitionSpec as P

BLK = 64
LOG2E = 1.4426950408889634


def block_terms(row_data, small_data, key_rows, value_rows, own_shard, groups):
    count = row_data.shape[0]
    head_size = key_rows.shape[1]
    per_shard = key_rows.shape[0] // BLK
    queries = row_data[:, :head_size]
    grads = row_data[:, head_size:]
    stats = small_data[:, :2].astype(jnp.float32)
    shards_of = small_data[:, 2 : 2 + groups].astype(jnp.int32)
    picks_of = small_data[:, 2 + groups :].astype(jnp.int32).reshape(count, groups, -1)
    local_ids = jnp.arange(per_shard, dtype=jnp.int32)
    matched = (shards_of == own_shard + 1)[:, :, None, None] & (
        picks_of[:, :, :, None] == local_ids[None, None, None, :]
    )
    chosen = jnp.any(matched, axis=(1, 2))
    mask = jnp.broadcast_to(chosen[:, :, None], (count, per_shard, BLK)).reshape(
        count, key_rows.shape[0]
    )
    scores = jnp.dot(queries, key_rows.T, preferred_element_type=jnp.float32) * head_size ** (-0.5)
    probs = jnp.where(mask, jnp.exp(scores - stats[:, 0:1]), 0.0)
    probs_low = probs.astype(jnp.bfloat16)
    value_add = jnp.dot(probs_low.T, grads, preferred_element_type=jnp.float32)
    dprob = jnp.dot(grads, value_rows.T, preferred_element_type=jnp.float32)
    dscore = (probs * (dprob - stats[:, 1:2])).astype(jnp.bfloat16)
    key_add = jnp.dot(dscore.T, queries, preferred_element_type=jnp.float32)
    query_part = jnp.dot(dscore, key_rows, preferred_element_type=jnp.float32)
    return (query_part, key_add, value_add)


def sweep(rows_in, small_in, key_rows, value_rows, own_shard, groups):
    sources, per_source = (rows_in.shape[0], rows_in.shape[1])
    merged = 1
    while merged * 2 <= sources and sources % (merged * 2) == 0 and (merged * per_source < 512):
        merged = merged * 2
    rows_blocks = rows_in.reshape(sources // merged, merged * per_source, rows_in.shape[2])
    small_blocks = small_in.reshape(sources // merged, merged * per_source, small_in.shape[2])
    zeros_kv = jnp.zeros(key_rows.shape, jnp.float32)

    def advance(carry, pieces):
        query_part, key_add, value_add = block_terms(
            pieces[0], pieces[1], key_rows, value_rows, own_shard, groups
        )
        return ((carry[0] + key_add, carry[1] + value_add), query_part)

    (key_sum, value_sum), query_parts = lax.scan(
        advance, (zeros_kv, zeros_kv), (rows_blocks, small_blocks)
    )
    return (query_parts.reshape(sources, per_source, -1), key_sum, value_sum)


def general_local(query_rows, key_rows, value_rows, attn_out, out_grad, logsumexp, shard_pick, block_pick):
    head_size = query_rows.shape[1]
    q_count = query_rows.shape[0]
    scale = head_size ** (-0.5)
    out_local, grad_local = (
        lax.all_to_all(attn_out, "head", split_axis=1, concat_axis=0, tiled=True),
        lax.all_to_all(out_grad, "head", split_axis=1, concat_axis=0, tiled=True),
    )
    delta = jnp.sum(
        out_local.astype(jnp.float32) * grad_local.astype(jnp.float32), axis=1, keepdims=True
    ).astype(jnp.bfloat16)
    seq_count = lax.axis_size("seq")
    own_shard = lax.axis_index("seq")
    targets = shard_pick[0]
    groups = targets.shape[1]
    picks = block_pick[0].reshape(q_count, -1)
    row_data = jnp.concatenate([query_rows, grad_local], axis=1)
    small_data = jnp.concatenate(
        [
            logsumexp[0][:, None],
            delta,
            (targets + 1).astype(jnp.bfloat16),
            picks.astype(jnp.bfloat16),
        ],
        axis=1,
    )
    capacity = min(q_count, 2 * q_count * groups // seq_count)
    shard_ids = jnp.arange(seq_count, dtype=jnp.int32)
    hits = jnp.any(targets[:, :, None] == shard_ids[None, None, :], axis=1).astype(jnp.float32)
    row_ids = jnp.arange(q_count, dtype=jnp.int32)
    lower = (row_ids[:, None] >= row_ids[None, :]).astype(jnp.float32)
    slots = (
        jnp.dot(lower, hits, precision=lax.Precision.HIGHEST, preferred_element_type=jnp.float32)
        - 1.0
    )
    slot_ids = jnp.arange(capacity, dtype=jnp.float32)
    dispatch = hits.T[:, None, :] * (slots.T[:, None, :] == slot_ids[None, :, None]).astype(
        jnp.float32
    )
    dispatch_low = dispatch.astype(jnp.bfloat16)
    send_rows = jnp.einsum(
        "scr,rf->scf", dispatch_low, row_data, preferred_element_type=jnp.float32
    ).astype(jnp.bfloat16)
    send_small = jnp.einsum(
        "scr,rf->scf", dispatch_low, small_data, preferred_element_type=jnp.float32
    ).astype(jnp.bfloat16)
    got_rows, got_small = (
        lax.all_to_all(send_rows, "seq", split_axis=0, concat_axis=0, tiled=True),
        lax.all_to_all(send_small, "seq", split_axis=0, concat_axis=0, tiled=True),
    )
    query_parts, key_sum, value_sum = sweep(
        got_rows, got_small, key_rows, value_rows, own_shard, groups
    )
    returned = lax.all_to_all(query_parts, "seq", split_axis=0, concat_axis=0, tiled=True)
    total = jnp.einsum(
        "scr,scd->rd",
        dispatch,
        returned,
        precision=lax.Precision.HIGHEST,
        preferred_element_type=jnp.float32,
    )
    query_grad = (total * scale).astype(jnp.bfloat16)
    key_grad = (key_sum * scale).astype(jnp.bfloat16)
    value_grad = value_sum.astype(jnp.bfloat16)
    return (query_grad, key_grad, value_grad)


def swap(value, axis, count, bit):
    return lax.ppermute(value, axis, [(i, i ^ bit) for i in range(count)])


def row_sums(left, right):
    product = left.astype(jnp.float32) * right.astype(jnp.float32)
    high = product.astype(jnp.bfloat16)
    low = (product - high.astype(jnp.float32)).astype(jnp.bfloat16)
    both = jnp.concatenate([high, low], axis=1)
    ones = jnp.ones((8, both.shape[1]), jnp.bfloat16)
    contract = (((1,), (1,)), ((), ()))
    return lax.dot_general(ones, both, contract, preferred_element_type=jnp.float32)[0:1]


def unpack(parts, count, times=1):
    queries, grads, outs = (
        jnp.concatenate([r[k * count : (k + 1) * count] for r in parts], axis=0) for k in range(3)
    )
    small = [r[3 * count : 4 * count].astype(jnp.float32) for r in parts]
    lane = lax.broadcasted_iota(jnp.int32, small[0].shape, 1) // count
    merged = small[0]
    for k in range(1, len(parts) * times):
        merged = jnp.where(lane == k, small[k % len(parts)], merged)
    half = merged.shape[0] // 2
    delta = row_sums(
        jnp.concatenate([outs] * times, axis=0), jnp.concatenate([grads] * times, axis=0)
    ).astype(jnp.bfloat16).astype(jnp.float32)
    return queries, grads, delta, merged[0:1], merged[half:]


def chosen_offset(lse, ids, blocks, base):
    number = lax.broadcasted_iota(jnp.int32, (blocks, ids.shape[1]), 0) + base
    number = number.astype(jnp.float32)
    chosen = ids[0:1] == number
    for k in range(1, ids.shape[0]):
        chosen = chosen | (ids[k : k + 1] == number)
    return jnp.where(chosen, lse * LOG2E, 1e30)


def terms(queries, grads, delta, offset, keys, values, scale):
    contract = (((1,), (1,)), ((), ()))
    scores = lax.dot_general(keys, queries, contract, preferred_element_type=jnp.float32)
    dprob = lax.dot_general(values, grads, contract, preferred_element_type=jnp.float32)
    scores = scores.reshape(offset.shape[0], BLK, -1)
    probs = jnp.exp2(scores * (scale * LOG2E) - offset[:, None, :]).reshape(dprob.shape)
    return probs, probs * (dprob - delta)


def doubled(r0, r1):
    parts, count = (r0[...], r1[...]), r0.shape[0] // 4
    queries, grads, delta, lse, ids = unpack(parts, count, 2)

    def beside(value):
        zero = jnp.zeros_like(value)
        left, right = jnp.concatenate([value, zero], axis=1), jnp.concatenate([zero, value], axis=1)
        return jnp.concatenate([left, right], axis=0)

    return beside(queries), beside(grads), delta, lse, ids


def rows_kernel(r0, r1, queries, grads, stats):
    queries[...], grads[...], delta, lse, ids = doubled(r0, r1)
    stats[0:1], stats[1:2], stats[8:] = delta, lse, ids


def query_kernel(
    scale, shard_ref, queries, grads, stats, k0, v0, k1, v1, k2, v2, k3, v3, q_own, q_out
):
    half, size, count = queries.shape[0] // 2, queries.shape[1] // 2, q_own.shape[0]
    delta, lse, ids = stats[0:1], stats[1:2], stats[8:]
    lane = lax.broadcasted_iota(jnp.int32, (1, 2 * half), 1)
    wide, scored = [], []
    for bit, left, right in ((0, (k0, v0), (k1, v1)), (2, (k2, v2), (k3, v3))):
        keys = jnp.concatenate([left[0][...], right[0][...]], axis=1)
        values = jnp.concatenate([left[1][...], right[1][...]], axis=1)
        blocks = keys.shape[0] // BLK
        base = jnp.where(lane < half, shard_ref[0] ^ bit, shard_ref[0] ^ (bit + 1)) * blocks
        offset = chosen_offset(lse, ids, blocks, base)
        _, dscore = terms(queries[...], grads[...], delta, offset, keys, values, scale)
        wide.append(keys)
        scored.append(dscore.T.astype(jnp.bfloat16))
    scored, wide = jnp.concatenate(scored, axis=1), jnp.concatenate(wide, axis=0)
    total = jnp.dot(scored, wide, preferred_element_type=jnp.float32)
    total = total[:half, :size] + total[half:, size:]
    q_own[...] = total[:count]
    q_out[...] = total[count:].astype(q_out.dtype)


def key_sums(shard, parts, keys, values, scale):
    count = parts[0].shape[0] // 4
    queries, grads, delta, lse, ids = unpack(parts, count)
    blocks = keys.shape[0] // BLK
    offset = chosen_offset(lse, ids, blocks, shard * blocks)
    probs, dscore = terms(queries, grads, delta, offset, keys, values, scale)
    low = jnp.bfloat16
    v_sum = jnp.dot(probs.astype(low), grads, preferred_element_type=jnp.float32)
    k_sum = jnp.dot(dscore.astype(low), queries, preferred_element_type=jnp.float32)
    return k_sum, v_sum


def key_kernel(scale, shard_ref, lane, keys, values, k_part, v_part):
    parts = [lane[k] for k in range(lane.shape[0])]
    k_part[...], v_part[...] = key_sums(shard_ref[0], parts, keys[...], values[...], scale)


def query_sum_kernel(scale, q_own, q_back, q_sum):
    q_sum[...] = ((q_own[...] + q_back[...].astype(jnp.float32)) * scale).astype(q_sum.dtype)


def finish_kernel(
    scale, shard_ref, lane, keys, values, k_part, v_part, q_sum, q_out, k_out, v_out
):
    parts = [lane[k] for k in range(lane.shape[0])]
    k_sum, v_sum = key_sums(shard_ref[0], parts, keys[...], values[...], scale)
    k_out[...] = ((k_sum + k_part[...]) * scale).astype(k_out.dtype)
    v_out[...] = (v_sum + v_part[...]).astype(v_out.dtype)
    q_out[...] = q_sum[...]


def small_kernel(blocks_dev, queries, lse, shards, picks, early):
    count, size = queries.shape
    row = lax.broadcasted_iota(jnp.int32, (count, size), 0)
    lane = lax.broadcasted_iota(jnp.int32, (count, size), 1)
    repeat = (lane % count == row).astype(jnp.bfloat16)
    ids = [shards[g : g + 1] * blocks_dev + picks[g] for g in range(shards.shape[0])]
    ids = jnp.concatenate(ids, axis=0).astype(jnp.float32)
    stats = jnp.broadcast_to(lse[...].astype(jnp.float32), ids.shape)
    both = jnp.concatenate([stats, ids], axis=0).astype(jnp.bfloat16)
    early[:count] = queries[...]
    both = jnp.dot(both, repeat, preferred_element_type=jnp.float32)
    early[count:] = both.astype(early.dtype)


def fast_local(query_rows, key_rows, value_rows, attn_out, out_grad, logsumexp, shard_pick, block_pick):
    count, size = query_rows.shape
    kv = key_rows.shape
    n_seq, n_head = lax.axis_size("seq"), lax.axis_size("head")
    seq, head = lax.axis_index("seq"), lax.axis_index("head")
    scale = size ** (-0.5)
    f32, bf16 = jnp.float32, jnp.bfloat16
    vmem = pl.BlockSpec(memory_space=pltpu.VMEM)
    smem = pl.BlockSpec(memory_space=pltpu.SMEM)

    def kernel(body, name, outs, scalars, args, flops=None, last=False):
        cost = None
        if flops is not None:
            cost = pl.CostEstimate(
                flops=flops, bytes_accessed=max(flops // 1000, 1), transcendentals=0
            )
        return pl.pallas_call(
            body,
            out_shape=tuple(jax.ShapeDtypeStruct(v, t) for v, t in outs),
            in_specs=[smem] * len(scalars) + [vmem] * len(args),
            compiler_params=pltpu.CompilerParams(vmem_limit_bytes=32 * 1024 * 1024),
            cost_estimate=cost,
            name=name,
            **({} if last else dict(out_specs=(vmem,) * len(outs))),
        )(*(v[None].astype(jnp.int32) for v in scalars), *args)

    mine = jnp.stack([out_grad, attn_out])
    near = swap(mine, "head", n_head, 1)
    mine, keys, values = lax.optimization_barrier((mine, key_rows, value_rows))
    keys_side = swap(keys, "seq", n_seq, 2)
    values_side = swap(values, "seq", n_seq, 2)
    near, shard_pick, block_pick, query_rows, logsumexp = lax.optimization_barrier(
        (near, shard_pick, block_pick, query_rows, logsumexp)
    )

    def pieces(which):
        both = jnp.stack([mine, near], axis=1)
        return lax.dynamic_slice_in_dim(both, which * size, size, axis=3)

    here = pieces(head)
    other = swap(pieces(head ^ 2), "head", n_head, 2)
    near, keys, values = lax.optimization_barrier((near, key_rows, value_rows))
    keys_core = swap(keys, "seq", n_seq, 1)
    values_core = swap(values, "seq", n_seq, 1)
    keys_side_core = swap(keys_side, "seq", n_seq, 1)
    values_side_core = swap(values_side, "seq", n_seq, 1)
    (early,) = kernel(
        functools.partial(small_kernel, kv[0] // BLK), "small", [((2 * count, size), bf16)], (),
        (query_rows, logsumexp, shard_pick[0].T, block_pick[0].transpose(1, 2, 0)), flops=10**9,
    )
    early, other = lax.optimization_barrier((early, other))
    odd, high = (head & 1) == 1, (head & 2) == 2
    both = jnp.stack([jnp.where(high, other, here), jnp.where(high, here, other)], axis=1)
    both = jnp.where(odd, both[:, :, ::-1], both)
    both = both.reshape(2 * count, size)
    block = jnp.concatenate([early[:count], both, early[count:]], axis=0)
    block, keys_core, values_core = lax.optimization_barrier((block, keys_core, values_core))
    block_y = swap(block, "seq", n_seq, 4)
    block_x = swap(block, "seq", n_seq, 2)
    block_d = swap(block, "seq", n_seq, 6)
    wide = (4 * count, 2 * size)
    rows = kernel(
        rows_kernel, "rows", [(wide, bf16), (wide, bf16), ((24, 4 * count), f32)], (),
        (block, block_y), flops=10**11,
    )
    q_own, q_out = kernel(
        functools.partial(query_kernel, scale), "query_terms",
        [((count, size), f32), ((count, size), bf16)], (seq,),
        (*rows, key_rows, value_rows, keys_core, values_core)
        + (keys_side, values_side, keys_side_core, values_side_core),
        flops=1,
    )
    _, block_x, block_d = lax.optimization_barrier((q_out, block_x, block_d))
    q_back = swap(q_out, "seq", n_seq, 4)
    lane = jnp.stack([block, block_y, block_x, block_d])
    lane_core = swap(lane, "seq", n_seq, 1)
    k_part, v_part = kernel(
        functools.partial(key_kernel, scale), "key_terms", [(kv, f32)] * 2, (seq,),
        (lane, key_rows, value_rows), flops=3 * 10**9,
    )
    (q_sum,) = kernel(
        functools.partial(query_sum_kernel, scale), "query_sum", [((count, size), bf16)], (),
        (q_own, q_back), flops=10**9,
    )
    return kernel(
        functools.partial(finish_kernel, scale), "finish",
        [((count, size), bf16), (kv, bf16), (kv, bf16)], (seq,),
        (lane_core, key_rows, value_rows, k_part, v_part, q_sum), last=True,
    )


def solution(mesh):
    placed = (
        P("seq", "head"),
        P("seq", "head"),
        P("seq", "head"),
        P(("seq", "head"), None),
        P(("seq", "head"), None),
        P("head", "seq"),
        P("head", "seq", None),
        P("head", "seq", None, None),
    )
    small = mesh.shape["seq"] == 8 and mesh.shape["head"] == 4

    def local(*args):
        count, size = args[0].shape
        fits = small and count * 4 == size == 128 and args[7].shape[2] * args[7].shape[3] == 16
        return (fast_local if fits else general_local)(*args)

    return jax.shard_map(
        local,
        mesh=mesh,
        in_specs=placed,
        out_specs=(P("seq", "head"), P("seq", "head"), P("seq", "head")),
        check_vma=False,
    )
```

```python
import functools

import jax
import jax.numpy as jnp
from jax import lax
from jax.experimental import pallas as pl
from jax.experimental.pallas import tpu as pltpu
from jax.sharding import PartitionSpec as P

BLK = 64
LOG2E = 1.4426950408889634


def block_terms(row_data, small_data, key_rows, value_rows, own_shard, groups):
    count = row_data.shape[0]
    head_size = key_rows.shape[1]
    per_shard = key_rows.shape[0] // BLK
    queries = row_data[:, :head_size]
    grads = row_data[:, head_size:]
    stats = small_data[:, :2].astype(jnp.float32)
    shards_of = small_data[:, 2 : 2 + groups].astype(jnp.int32)
    picks_of = small_data[:, 2 + groups :].astype(jnp.int32).reshape(count, groups, -1)
    local_ids = jnp.arange(per_shard, dtype=jnp.int32)
    matched = (shards_of == own_shard + 1)[:, :, None, None] & (
        picks_of[:, :, :, None] == local_ids[None, None, None, :]
    )
    chosen = jnp.any(matched, axis=(1, 2))
    mask = jnp.broadcast_to(chosen[:, :, None], (count, per_shard, BLK)).reshape(
        count, key_rows.shape[0]
    )
    scores = jnp.dot(queries, key_rows.T, preferred_element_type=jnp.float32) * head_size ** (-0.5)
    probs = jnp.where(mask, jnp.exp(scores - stats[:, 0:1]), 0.0)
    probs_low = probs.astype(jnp.bfloat16)
    value_add = jnp.dot(probs_low.T, grads, preferred_element_type=jnp.float32)
    dprob = jnp.dot(grads, value_rows.T, preferred_element_type=jnp.float32)
    dscore = (probs * (dprob - stats[:, 1:2])).astype(jnp.bfloat16)
    key_add = jnp.dot(dscore.T, queries, preferred_element_type=jnp.float32)
    query_part = jnp.dot(dscore, key_rows, preferred_element_type=jnp.float32)
    return (query_part, key_add, value_add)


def sweep(rows_in, small_in, key_rows, value_rows, own_shard, groups):
    sources, per_source = (rows_in.shape[0], rows_in.shape[1])
    merged = 1
    while merged * 2 <= sources and sources % (merged * 2) == 0 and (merged * per_source < 512):
        merged = merged * 2
    rows_blocks = rows_in.reshape(sources // merged, merged * per_source, rows_in.shape[2])
    small_blocks = small_in.reshape(sources // merged, merged * per_source, small_in.shape[2])
    zeros_kv = jnp.zeros(key_rows.shape, jnp.float32)

    def advance(carry, pieces):
        query_part, key_add, value_add = block_terms(
            pieces[0], pieces[1], key_rows, value_rows, own_shard, groups
        )
        return ((carry[0] + key_add, carry[1] + value_add), query_part)

    (key_sum, value_sum), query_parts = lax.scan(
        advance, (zeros_kv, zeros_kv), (rows_blocks, small_blocks)
    )
    return (query_parts.reshape(sources, per_source, -1), key_sum, value_sum)


def general_local(query_rows, key_rows, value_rows, attn_out, out_grad, logsumexp, shard_pick, block_pick):
    head_size = query_rows.shape[1]
    q_count = query_rows.shape[0]
    scale = head_size ** (-0.5)
    out_local, grad_local = (
        lax.all_to_all(attn_out, "head", split_axis=1, concat_axis=0, tiled=True),
        lax.all_to_all(out_grad, "head", split_axis=1, concat_axis=0, tiled=True),
    )
    delta = jnp.sum(
        out_local.astype(jnp.float32) * grad_local.astype(jnp.float32), axis=1, keepdims=True
    ).astype(jnp.bfloat16)
    seq_count = lax.axis_size("seq")
    own_shard = lax.axis_index("seq")
    targets = shard_pick[0]
    groups = targets.shape[1]
    picks = block_pick[0].reshape(q_count, -1)
    row_data = jnp.concatenate([query_rows, grad_local], axis=1)
    small_data = jnp.concatenate(
        [
            logsumexp[0][:, None],
            delta,
            (targets + 1).astype(jnp.bfloat16),
            picks.astype(jnp.bfloat16),
        ],
        axis=1,
    )
    capacity = min(q_count, 2 * q_count * groups // seq_count)
    shard_ids = jnp.arange(seq_count, dtype=jnp.int32)
    hits = jnp.any(targets[:, :, None] == shard_ids[None, None, :], axis=1).astype(jnp.float32)
    row_ids = jnp.arange(q_count, dtype=jnp.int32)
    lower = (row_ids[:, None] >= row_ids[None, :]).astype(jnp.float32)
    slots = (
        jnp.dot(lower, hits, precision=lax.Precision.HIGHEST, preferred_element_type=jnp.float32)
        - 1.0
    )
    slot_ids = jnp.arange(capacity, dtype=jnp.float32)
    dispatch = hits.T[:, None, :] * (slots.T[:, None, :] == slot_ids[None, :, None]).astype(
        jnp.float32
    )
    dispatch_low = dispatch.astype(jnp.bfloat16)
    send_rows = jnp.einsum(
        "scr,rf->scf", dispatch_low, row_data, preferred_element_type=jnp.float32
    ).astype(jnp.bfloat16)
    send_small = jnp.einsum(
        "scr,rf->scf", dispatch_low, small_data, preferred_element_type=jnp.float32
    ).astype(jnp.bfloat16)
    got_rows, got_small = (
        lax.all_to_all(send_rows, "seq", split_axis=0, concat_axis=0, tiled=True),
        lax.all_to_all(send_small, "seq", split_axis=0, concat_axis=0, tiled=True),
    )
    query_parts, key_sum, value_sum = sweep(
        got_rows, got_small, key_rows, value_rows, own_shard, groups
    )
    returned = lax.all_to_all(query_parts, "seq", split_axis=0, concat_axis=0, tiled=True)
    total = jnp.einsum(
        "scr,scd->rd",
        dispatch,
        returned,
        precision=lax.Precision.HIGHEST,
        preferred_element_type=jnp.float32,
    )
    query_grad = (total * scale).astype(jnp.bfloat16)
    key_grad = (key_sum * scale).astype(jnp.bfloat16)
    value_grad = value_sum.astype(jnp.bfloat16)
    return (query_grad, key_grad, value_grad)


def swap(value, axis, count, bit):
    return lax.ppermute(value, axis, [(i, i ^ bit) for i in range(count)])


def row_sums(left, right):
    product = left.astype(jnp.float32) * right.astype(jnp.float32)
    high = product.astype(jnp.bfloat16)
    low = (product - high.astype(jnp.float32)).astype(jnp.bfloat16)
    both = jnp.concatenate([high, low], axis=1)
    ones = jnp.ones((8, both.shape[1]), jnp.bfloat16)
    contract = (((1,), (1,)), ((), ()))
    return lax.dot_general(ones, both, contract, preferred_element_type=jnp.float32)[0:1]


def unpack(parts, count, times=1):
    queries, grads, outs = (
        jnp.concatenate([r[k * count : (k + 1) * count] for r in parts], axis=0) for k in range(3)
    )
    small = [r[3 * count : 4 * count] for r in parts]
    lane = lax.broadcasted_iota(jnp.int32, small[0].shape, 1) // count
    merged = small[0]
    for k in range(1, len(parts) * times):
        merged = jnp.where(lane == k, small[k % len(parts)], merged)
    merged = merged.astype(jnp.float32)
    half = merged.shape[0] // 2
    delta = row_sums(
        jnp.concatenate([outs] * times, axis=0), jnp.concatenate([grads] * times, axis=0)
    ).astype(jnp.bfloat16).astype(jnp.float32)
    return queries, grads, delta, merged[0:1], merged[half:]


def chosen_offset(lse, ids, blocks, base):
    number = lax.broadcasted_iota(jnp.int32, (blocks, ids.shape[1]), 0) + base
    number = number.astype(jnp.float32)
    chosen = ids[0:1] == number
    for k in range(1, ids.shape[0]):
        chosen = chosen | (ids[k : k + 1] == number)
    return jnp.where(chosen, lse * LOG2E, 1e30)


def terms(queries, grads, delta, offset, keys, values, scale):
    contract = (((1,), (1,)), ((), ()))
    scores = lax.dot_general(keys, queries, contract, preferred_element_type=jnp.float32)
    dprob = lax.dot_general(values, grads, contract, preferred_element_type=jnp.float32)
    scores = scores.reshape(offset.shape[0], BLK, -1)
    probs = jnp.exp2(scores * (scale * LOG2E) - offset[:, None, :]).reshape(dprob.shape)
    return probs, probs * (dprob - delta)


def doubled(r0, r1):
    parts, count = (r0[...], r1[...]), r0.shape[0] // 4
    queries, grads, delta, lse, ids = unpack(parts, count, 2)

    def beside(value):
        zero = jnp.zeros_like(value)
        left, right = jnp.concatenate([value, zero], axis=1), jnp.concatenate([zero, value], axis=1)
        return jnp.concatenate([left, right], axis=0)

    return beside(queries), beside(grads), delta, lse, ids


def rows_kernel(r0, r1, queries, grads, stats):
    queries[...], grads[...], delta, lse, ids = doubled(r0, r1)
    stats[0:1], stats[1:2], stats[8:] = delta, lse, ids


def query_kernel(
    scale, shard_ref, queries, grads, stats, k0, v0, k1, v1, k2, v2, k3, v3, q_own, q_out
):
    half, size, count = queries.shape[0] // 2, queries.shape[1] // 2, q_own.shape[0]
    delta, lse, ids = stats[0:1], stats[1:2], stats[8:]
    lane = lax.broadcasted_iota(jnp.int32, (1, 2 * half), 1)
    wide, scored = [], []
    for bit, left, right in ((0, (k0, v0), (k1, v1)), (2, (k2, v2), (k3, v3))):
        keys = jnp.concatenate([left[0][...], right[0][...]], axis=1)
        values = jnp.concatenate([left[1][...], right[1][...]], axis=1)
        blocks = keys.shape[0] // BLK
        base = jnp.where(lane < half, shard_ref[0] ^ bit, shard_ref[0] ^ (bit + 1)) * blocks
        offset = chosen_offset(lse, ids, blocks, base)
        _, dscore = terms(queries[...], grads[...], delta, offset, keys, values, scale)
        wide.append(keys)
        scored.append(dscore.T.astype(jnp.bfloat16))
    scored, wide = jnp.concatenate(scored, axis=1), jnp.concatenate(wide, axis=0)
    total = jnp.dot(scored, wide, preferred_element_type=jnp.float32)
    total = total[:half, :size] + total[half:, size:]
    q_own[...] = total[:count]
    q_out[...] = total[count:].astype(q_out.dtype)


def key_sums(shard, parts, keys, values, scale):
    count = parts[0].shape[0] // 4
    queries, grads, delta, lse, ids = unpack(parts, count)
    blocks = keys.shape[0] // BLK
    offset = chosen_offset(lse, ids, blocks, shard * blocks)
    probs, dscore = terms(queries, grads, delta, offset, keys, values, scale)
    low = jnp.bfloat16
    v_sum = jnp.dot(probs.astype(low), grads, preferred_element_type=jnp.float32)
    k_sum = jnp.dot(dscore.astype(low), queries, preferred_element_type=jnp.float32)
    return k_sum, v_sum


def key_kernel(scale, shard_ref, lane, keys, values, k_part, v_part):
    parts = [lane[k] for k in range(lane.shape[0])]
    k_part[...], v_part[...] = key_sums(shard_ref[0], parts, keys[...], values[...], scale)


def query_sum_kernel(scale, q_own, q_back, q_sum):
    q_sum[...] = ((q_own[...] + q_back[...].astype(jnp.float32)) * scale).astype(q_sum.dtype)


def finish_kernel(
    scale, shard_ref, lane, keys, values, k_part, v_part, q_sum, q_out, k_out, v_out
):
    parts = [lane[k] for k in range(lane.shape[0])]
    k_sum, v_sum = key_sums(shard_ref[0], parts, keys[...], values[...], scale)
    k_out[...] = ((k_sum + k_part[...]) * scale).astype(k_out.dtype)
    v_out[...] = (v_sum + v_part[...]).astype(v_out.dtype)
    q_out[...] = q_sum[...]


def small_kernel(blocks_dev, queries, lse, shards, picks, early):
    count, size = queries.shape
    row = lax.broadcasted_iota(jnp.int32, (count, size), 0)
    lane = lax.broadcasted_iota(jnp.int32, (count, size), 1)
    repeat = (lane % count == row).astype(jnp.bfloat16)
    ids = [shards[g : g + 1] * blocks_dev + picks[g] for g in range(shards.shape[0])]
    ids = jnp.concatenate(ids, axis=0).astype(jnp.float32)
    stats = jnp.broadcast_to(lse[...].astype(jnp.float32), ids.shape)
    both = jnp.concatenate([stats, ids], axis=0).astype(jnp.bfloat16)
    early[:count] = queries[...]
    both = jnp.dot(both, repeat, preferred_element_type=jnp.float32)
    early[count:] = both.astype(early.dtype)


def fast_local(query_rows, key_rows, value_rows, attn_out, out_grad, logsumexp, shard_pick, block_pick):
    count, size = query_rows.shape
    kv = key_rows.shape
    n_seq, n_head = lax.axis_size("seq"), lax.axis_size("head")
    seq, head = lax.axis_index("seq"), lax.axis_index("head")
    scale = size ** (-0.5)
    f32, bf16 = jnp.float32, jnp.bfloat16
    vmem = pl.BlockSpec(memory_space=pltpu.VMEM)
    smem = pl.BlockSpec(memory_space=pltpu.SMEM)

    def kernel(body, name, outs, scalars, args, flops=None, last=False):
        cost = None
        if flops is not None:
            cost = pl.CostEstimate(
                flops=flops, bytes_accessed=max(flops // 1000, 1), transcendentals=0
            )
        return pl.pallas_call(
            body,
            out_shape=tuple(jax.ShapeDtypeStruct(v, t) for v, t in outs),
            in_specs=[smem] * len(scalars) + [vmem] * len(args),
            compiler_params=pltpu.CompilerParams(vmem_limit_bytes=32 * 1024 * 1024),
            cost_estimate=cost,
            name=name,
            **({} if last else dict(out_specs=(vmem,) * len(outs))),
        )(*(v[None].astype(jnp.int32) for v in scalars), *args)

    mine = jnp.stack([out_grad, attn_out])
    near = swap(mine, "head", n_head, 1)
    mine, keys, values = lax.optimization_barrier((mine, key_rows, value_rows))
    keys_side = swap(keys, "seq", n_seq, 2)
    values_side = swap(values, "seq", n_seq, 2)
    near, shard_pick, block_pick, query_rows, logsumexp = lax.optimization_barrier(
        (near, shard_pick, block_pick, query_rows, logsumexp)
    )

    def pieces(which):
        both = jnp.stack([mine, near], axis=1)
        return lax.dynamic_slice_in_dim(both, which * size, size, axis=3)

    here = pieces(head)
    other = swap(pieces(head ^ 2), "head", n_head, 2)
    near, keys, values = lax.optimization_barrier((near, key_rows, value_rows))
    keys_core = swap(keys, "seq", n_seq, 1)
    values_core = swap(values, "seq", n_seq, 1)
    keys_side_core = swap(keys_side, "seq", n_seq, 1)
    values_side_core = swap(values_side, "seq", n_seq, 1)
    (early,) = kernel(
        functools.partial(small_kernel, kv[0] // BLK), "small", [((2 * count, size), bf16)], (),
        (query_rows, logsumexp, shard_pick[0].T, block_pick[0].transpose(1, 2, 0)), flops=10**9,
    )
    early, other = lax.optimization_barrier((early, other))
    odd, high = (head & 1) == 1, (head & 2) == 2
    both = jnp.stack([jnp.where(high, other, here), jnp.where(high, here, other)], axis=1)
    both = jnp.where(odd, both[:, :, ::-1], both)
    both = both.reshape(2 * count, size)
    block = jnp.concatenate([early[:count], both, early[count:]], axis=0)
    block, keys_core, values_core = lax.optimization_barrier((block, keys_core, values_core))
    block_y = swap(block, "seq", n_seq, 4)
    block_x = swap(block, "seq", n_seq, 2)
    block_d = swap(block, "seq", n_seq, 6)
    wide = (4 * count, 2 * size)
    rows = kernel(
        rows_kernel, "rows", [(wide, bf16), (wide, bf16), ((24, 4 * count), f32)], (),
        (block, block_y), flops=10**11,
    )
    q_own, q_out = kernel(
        functools.partial(query_kernel, scale), "query_terms",
        [((count, size), f32), ((count, size), bf16)], (seq,),
        (*rows, key_rows, value_rows, keys_core, values_core)
        + (keys_side, values_side, keys_side_core, values_side_core),
        flops=1,
    )
    _, block_x, block_d = lax.optimization_barrier((q_out, block_x, block_d))
    q_back = swap(q_out, "seq", n_seq, 4)
    lane = jnp.stack([block, block_y, block_x, block_d])
    lane_core = swap(lane, "seq", n_seq, 1)
    k_part, v_part = kernel(
        functools.partial(key_kernel, scale), "key_terms", [(kv, f32)] * 2, (seq,),
        (lane, key_rows, value_rows), flops=3 * 10**9,
    )
    (q_sum,) = kernel(
        functools.partial(query_sum_kernel, scale), "query_sum", [((count, size), bf16)], (),
        (q_own, q_back), flops=10**9,
    )
    return kernel(
        functools.partial(finish_kernel, scale), "finish",
        [((count, size), bf16), (kv, bf16), (kv, bf16)], (seq,),
        (lane_core, key_rows, value_rows, k_part, v_part, q_sum), last=True,
    )


def solution(mesh):
    placed = (
        P("seq", "head"),
        P("seq", "head"),
        P("seq", "head"),
        P(("seq", "head"), None),
        P(("seq", "head"), None),
        P("head", "seq"),
        P("head", "seq", None),
        P("head", "seq", None, None),
    )
    small = mesh.shape["seq"] == 8 and mesh.shape["head"] == 4

    def local(*args):
        count, size = args[0].shape
        fits = small and count * 4 == size == 128 and args[7].shape[2] * args[7].shape[3] == 16
        return (fast_local if fits else general_local)(*args)

    return jax.shard_map(
        local,
        mesh=mesh,
        in_specs=placed,
        out_specs=(P("seq", "head"), P("seq", "head"), P("seq", "head")),
        check_vma=False,
    )
```
